32 devices in a mesh: dp: 4 (over y, core), cent: 8 (over z, x).
Axes of the slice: x: 2, y: 2, z: 4, core: 2. Of those that a mesh axis runs over, the one named last changes fastest.
Arguments:
- passages: bfloat16 [4096, 768], P(('dp', 'cent')), may hold values from -10 to 10
- queries: bfloat16 [128, 768], P(('dp', 'cent')), may hold values from -10 to 10
- init_centroids: float32 [2048, 768], P('cent'), may hold values from -12 to 12
- pattern: int32 [128, 4], replicated, may hold values from 0 to 31, all different within a row
- positive_offset: int32 [128], replicated, may hold values from 0 to 127
Outputs:
- centroids: float32 [2048, 768], P('cent')
- loss: float32 [128], P(('dp', 'cent'))
The draws below stay inside these ranges and needn't reach their ends.
Inputs may be any that keep to these rules, and one draw needn't show every extreme that they name: `pattern`: each row names 4 different blocks.
All inputs are finite; a program needn't handle non-finite values.
Results may differ from the reference program's by a relative error of at most 0.0055.
Values may be sent and summed in bfloat16 or wider, within the bound.
No kernel may reach another device: no remote copies, remote signals or barrier semaphores. Data moves between devices by JAX's collectives and lax.ppermute only.
A program may use at most 64 MiB of HBM per device.

```python
import jax
import jax.numpy as jnp
from jax import lax

D = 768
P_DEV = 128
BLOCK = 128
NB = 4
ITERS = 2
CENTERS = 2048
PASSAGES = 4096
QUERIES = 128
NBLK = 32
N_CENT = 8


def draw_passages(key, part):
    drawn_rows = jnp.clip(jax.random.normal(jax.random.fold_in(key, 1), (PASSAGES, D), jnp.float32), -6.0, 6.0)
    return drawn_rows.astype(jnp.bfloat16)


def draw_queries(key, part):
    drawn_rows = jnp.clip(jax.random.normal(jax.random.fold_in(key, 3), (QUERIES, D), jnp.float32), -6.0, 6.0)
    return drawn_rows.astype(jnp.bfloat16)


def draw_init_centroids(key, part):
    drawn_rows = jnp.clip(jax.random.normal(jax.random.fold_in(key, 2), (CENTERS, D), jnp.float32), -6.0, 6.0)
    return drawn_rows


def with_ends(result, key, low, high):
    index_at = [jax.random.randint(jax.random.fold_in(key, axis), (), 0, length) for axis, length in enumerate(result.shape)]
    longest = result.shape.index(max(result.shape))
    next_to = index_at[:longest] + [(index_at[longest] + 1) % result.shape[longest]] + index_at[longest + 1:]
    return result.at[tuple(index_at)].set(low).at[tuple(next_to)].set(high)


def distinct(own_key, rows, number_of, top, lift):
    sequence = jax.random.permutation(jax.random.fold_in(own_key, 1), number_of)
    boost = sequence
    for power in range(3):
        boost = boost * boost // number_of
    boost = boost * lift // number_of
    tickets = jax.random.randint(jax.random.fold_in(own_key, 2), (rows, number_of), 0, 4096) + boost
    holders = jax.random.permutation(jax.random.fold_in(own_key, 3), rows)[jnp.arange(number_of) % rows]
    tickets = jnp.where(jnp.arange(rows)[:, None] == holders[None, :], 1 << 14, tickets)
    priority = tickets * number_of + jnp.arange(number_of)
    return lax.top_k(priority.astype(jnp.int32), top)[1].astype(jnp.int32)


def setup_inputs(seed: int = 0) -> dict:
    keys = jax.random.split(jax.random.key(seed), 6)
    passages = draw_passages(jax.random.fold_in(keys[5], 71), 0)
    queries = draw_queries(jax.random.fold_in(keys[5], 71), 0)
    init_centroids = draw_init_centroids(jax.random.fold_in(keys[5], 71), 0)
    pattern = distinct(keys[3], QUERIES, NBLK, NB, 2048)
    positive_offset = with_ends(jax.random.randint(keys[4], (QUERIES,), 0, BLOCK), jax.random.fold_in(keys[4], 1), 0, BLOCK - 1).astype(jnp.int32)
    return dict(passages=passages, queries=queries, init_centroids=init_centroids, pattern=pattern, positive_offset=positive_offset)


sharpness = 0.05
sharpening_factor = 0.05
prior_weight = 1.0


def reference(passages, queries, init_centroids, pattern, positive_offset):
    cluster_means = init_centroids
    row_groups = passages.reshape(-1, P_DEV * N_CENT, D)
    for step_index in range(ITERS):
        centers_half = cluster_means.astype(jnp.bfloat16)
        cluster_center_norms = jnp.sum(cluster_means * cluster_means, axis=1)

        def group_terms(rows):
            unnormalized_log_odds = sharpness * (2.0 * jnp.dot(rows, centers_half.T, preferred_element_type=jnp.float32) - cluster_center_norms[None, :])
            resp = jax.nn.softmax(unnormalized_log_odds, axis=1)
            numer = jnp.dot(resp.astype(jnp.bfloat16).T, rows, preferred_element_type=jnp.float32)
            return numer, jnp.sum(resp, axis=0)

        numer_all, counts_all = lax.map(group_terms, row_groups)
        numer = jnp.sum(numer_all, axis=0)
        counts = jnp.sum(counts_all, axis=0)
        cluster_means = (numer + prior_weight * cluster_means) / (counts[:, None] + prior_weight)
    blocks = passages.reshape(NBLK, BLOCK, D)
    width = min(256, QUERIES)

    def query_terms(packed):
        question_tile_slice, picks, block_offsets = packed
        chosen_topic_label = blocks[picks]
        affinity_matrix = jnp.einsum("mz,mxdz->mxd", question_tile_slice.astype(jnp.float32), chosen_topic_label.astype(jnp.float32)) * sharpening_factor
        total = jax.scipy.special.logsumexp(affinity_matrix, axis=(1, 2))
        positive = jnp.take_along_axis(affinity_matrix[:, 0, :], block_offsets[:, None], axis=1)[:, 0]
        return total - positive

    losses = lax.map(query_terms, (queries.reshape(-1, width, D), pattern.reshape(-1, width, NB), positive_offset.reshape(-1, width)))
    return cluster_means, losses.reshape(QUERIES)
```

```python
import jax
import jax.numpy as jnp
from jax import lax
from jax.sharding import PartitionSpec as P

BLOCK = 128
ITERS = 2
SHARPNESS = 0.05
SCALE = 0.05
PRIOR = 1.0
FAR = -1e30


def swap(value, axis, bit):
    size = lax.axis_size(axis)
    return lax.ppermute(value, axis, [(i, i ^ bit) for i in range(size)])


def bits_of(size):
    return [1 << k for k in range(size.bit_length() - 1)]


def doubled(value, axis, order):
    for bit in order:
        value = jnp.stack([value, swap(value, axis, bit)])
    return value


def join_lse(first, second):
    top = jnp.maximum(first, second)
    return top + jnp.log(1.0 + jnp.exp(jnp.minimum(first, second) - top))


def on_device(passages, queries, init_centroids, pattern, positive_offset):
    n_dp, n_cent = lax.axis_size("dp"), lax.axis_size("cent")
    dp, cent = lax.axis_index("dp"), lax.axis_index("cent")
    dp_bits, cent_bits = bits_of(n_dp), bits_of(n_cent)
    rows, width = passages.shape
    own_queries = queries.shape[0]

    half = rows // 2
    orders = [cent_bits[1:] + cent_bits[:1], cent_bits]
    parts = [
        doubled(passages[:half], "cent", orders[0]),
        doubled(passages[half:], "cent", orders[1]),
    ]
    held = [part.reshape(-1, width) for part in parts]

    asked = queries
    for bit in dp_bits:
        other = swap(asked, "dp", bit)
        low = (dp & bit) == 0
        asked = jnp.concatenate([jnp.where(low, asked, other), jnp.where(low, other, asked)])

    core = dp & 1
    means = init_centroids
    kept = means.shape[0] // 2
    for step in range(ITERS):
        centers_half = means.astype(jnp.bfloat16)
        norms = jnp.sum(means * means, axis=1)
        odds, stats = [], []
        for index in range(2):
            logits = SHARPNESS * (
                2.0
                * lax.dot_general(
                    centers_half, held[index], (((1,), (1,)), ((), ())), preferred_element_type=jnp.float32
                )
                - norms[:, None]
            )
            top = jnp.max(logits, axis=0)
            odds.append(logits)
            stats.append(top + jnp.log(jnp.sum(jnp.exp(logits - top[None, :]), axis=0)))
        shape = (2,) * len(cent_bits) + (half,)
        views = []
        for index in range(2):
            view = stats[index].reshape(shape)
            axes = [len(cent_bits) - 1 - orders[index].index(bit) for bit in cent_bits]
            views.append(jnp.transpose(view, axes + [len(cent_bits)]))
        lse = jnp.concatenate(views, axis=-1)
        for position, bit in enumerate(cent_bits):
            lse = join_lse(lse, jnp.flip(swap(lse, "cent", bit), axis=position))
        numer, counts = 0.0, 0.0
        for index in range(2):
            view = lse[..., index * half : (index + 1) * half]
            axes = [cent_bits.index(bit) for bit in reversed(orders[index])]
            total = jnp.transpose(view, axes + [len(cent_bits)]).reshape(-1)
            resp = jnp.exp(odds[index] - total[None, :])
            counts = counts + jnp.sum(resp, axis=1)
            numer = numer + jnp.dot(
                resp.astype(jnp.bfloat16), held[index], preferred_element_type=jnp.float32
            )
        for bit in dp_bits:
            counts = counts + swap(counts, "dp", bit)
        pair = numer.reshape(2, kept, width)
        mine = lax.dynamic_index_in_dim(pair, core, 0, keepdims=False)
        mine = mine + swap(lax.dynamic_index_in_dim(pair, 1 - core, 0, keepdims=False), "dp", 1)
        for bit in dp_bits[1:]:
            sent = mine.astype(jnp.bfloat16)
            mine = sent.astype(jnp.float32) + swap(sent, "dp", bit).astype(jnp.float32)
        prior = lax.dynamic_slice_in_dim(means, core * kept, kept, 0)
        weight = lax.dynamic_slice_in_dim(counts, core * kept, kept, 0)
        fresh = (mine + PRIOR * prior) / (weight[:, None] + PRIOR)
        other = swap(fresh, "dp", 1)
        means = jnp.concatenate([jnp.where(core == 0, fresh, other), jnp.where(core == 0, other, fresh)])

    losses = []
    ids = ((jnp.arange(n_dp) * n_cent + cent) * own_queries)[:, None] + jnp.arange(own_queries)[None, :]
    ids = ids.reshape(-1)
    picks = pattern[ids]
    target = picks[:, 0] * BLOCK + positive_offset[ids]
    partial, positive = None, 0.0
    for index in range(2):
        where_bits = jnp.zeros((2,) * len(cent_bits), jnp.int32) + cent
        for bit in cent_bits:
            axis = len(cent_bits) - 1 - orders[index].index(bit)
            flag = lax.broadcasted_iota(jnp.int32, where_bits.shape, axis) * bit
            where_bits = where_bits ^ flag
        owner = (dp * n_cent + where_bits)[..., None] * rows
        column = (owner + index * half + jnp.arange(half, dtype=jnp.int32)).reshape(-1)
        scores = SCALE * lax.dot_general(
            asked, held[index], (((1,), (1,)), ((), ())), preferred_element_type=jnp.float32
        )
        allowed = jnp.any(picks[:, :, None] == (column // BLOCK)[None, None, :], axis=1)
        top = jnp.max(jnp.where(allowed, scores, FAR), axis=1)
        total = jnp.sum(jnp.where(allowed, jnp.exp(scores - top[:, None]), 0.0), axis=1)
        losses.append((top, total))
        positive = positive + jnp.sum(jnp.where(column[None, :] == target[:, None], scores, 0.0), axis=1)
    top = jnp.maximum(losses[0][0], losses[1][0])
    total = sum(t * jnp.exp(m - top) for m, t in losses)
    found = jnp.stack([jnp.where(total > 0.0, top + jnp.log(jnp.maximum(total, 1e-37)), FAR), positive])
    for bit in dp_bits:
        other = swap(found, "dp", bit)
        found = jnp.stack([join_lse(found[0], other[0]), found[1] + other[1]])
    whole = found[0] - found[1]
    loss = lax.dynamic_slice_in_dim(whole, dp * own_queries, own_queries, 0)
    return means, loss


def solution(mesh):
    placed = (P(("dp", "cent"), None), P(("dp", "cent"), None), P("cent", None), P(), P())
    return jax.shard_map(
        on_device,
        mesh=mesh,
        in_specs=placed,
        out_specs=(P("cent", None), P(("dp", "cent"))),
        check_vma=False,
    )
```

```python
import jax
import jax.numpy as jnp
from jax import lax
from jax.sharding import PartitionSpec as P

BLOCK = 128
ITERS = 2
SHARPNESS = 0.05
SCALE = 0.05
PRIOR = 1.0
FAR = -1e30


def swap(value, axis, bit):
    size = lax.axis_size(axis)
    return lax.ppermute(value, axis, [(i, i ^ bit) for i in range(size)])


def bits_of(size):
    return [1 << k for k in range(size.bit_length() - 1)]


def gathered_pieces(value, axis, size):
    pieces = {0: value}
    half = value.shape[0] // 2
    for mask in sorted(range(1, size), key=lambda m: (bin(m).count("1"), -m)):
        low = mask & -mask
        if bin(mask).count("1") < 3:
            pieces[mask] = swap(pieces[mask ^ low], axis, low)
        else:
            rest = mask ^ low
            second = rest & -rest
            pieces[mask] = jnp.concatenate(
                [swap(pieces[mask ^ low][:half], axis, low), swap(pieces[mask ^ second][half:], axis, second)]
            )
    return pieces


def join_lse(first, second):
    top = jnp.maximum(first, second)
    return top + jnp.log(1.0 + jnp.exp(jnp.minimum(first, second) - top))


def on_device(passages, queries, init_centroids, pattern, positive_offset):
    n_dp, n_cent = lax.axis_size("dp"), lax.axis_size("cent")
    dp, cent = lax.axis_index("dp"), lax.axis_index("cent")
    dp_bits, cent_bits = bits_of(n_dp), bits_of(n_cent)
    rows, width = passages.shape
    own_queries = queries.shape[0]

    pieces = gathered_pieces(passages, "cent", n_cent)
    half = n_cent // 2
    held = [
        jnp.concatenate([pieces[mask] for mask in range(start, start + half)]) for start in (0, half)
    ]

    asked = queries
    for bit in dp_bits:
        other = swap(asked, "dp", bit)
        low = (dp & bit) == 0
        asked = jnp.concatenate([jnp.where(low, asked, other), jnp.where(low, other, asked)])

    core = dp & 1
    means = init_centroids
    kept = means.shape[0] // 2
    for step in range(ITERS):
        centers_half = means.astype(jnp.bfloat16)
        norms = jnp.sum(means * means, axis=1)
        odds, stats = [], []
        for index in range(2):
            logits = SHARPNESS * (
                2.0
                * lax.dot_general(
                    centers_half, held[index], (((1,), (1,)), ((), ())), preferred_element_type=jnp.float32
                )
                - norms[:, None]
            )
            top = jnp.max(logits, axis=0)
            odds.append(logits)
            stats.append(top + jnp.log(jnp.sum(jnp.exp(logits - top[None, :]), axis=0)))
        lse = jnp.concatenate(stats).reshape((2,) * len(cent_bits) + (rows,))
        for bit in cent_bits:
            position = len(cent_bits) - 1 - cent_bits.index(bit)
            lse = join_lse(lse, jnp.flip(swap(lse, "cent", bit), axis=position))
        total = lse.reshape(2, half * rows)
        numer, counts = 0.0, 0.0
        for index in range(2):
            resp = jnp.exp(odds[index] - total[index][None, :])
            counts = counts + jnp.sum(resp, axis=1)
            numer = numer + jnp.dot(
                resp.astype(jnp.bfloat16), held[index], preferred_element_type=jnp.float32
            )
        for bit in dp_bits:
            counts = counts + swap(counts, "dp", bit)
        pair = numer.reshape(2, kept, width)
        mine = lax.dynamic_index_in_dim(pair, core, 0, keepdims=False)
        mine = mine + swap(lax.dynamic_index_in_dim(pair, 1 - core, 0, keepdims=False), "dp", 1)
        for bit in dp_bits[1:]:
            sent = mine.astype(jnp.bfloat16)
            mine = sent.astype(jnp.float32) + swap(sent, "dp", bit).astype(jnp.float32)
        prior = lax.dynamic_slice_in_dim(means, core * kept, kept, 0)
        weight = lax.dynamic_slice_in_dim(counts, core * kept, kept, 0)
        fresh = (mine + PRIOR * prior) / (weight[:, None] + PRIOR)
        other = swap(fresh, "dp", 1)
        means = jnp.concatenate([jnp.where(core == 0, fresh, other), jnp.where(core == 0, other, fresh)])

    losses = []
    ids = ((jnp.arange(n_dp) * n_cent + cent) * own_queries)[:, None] + jnp.arange(own_queries)[None, :]
    ids = ids.reshape(-1)
    picks = pattern[ids]
    target = picks[:, 0] * BLOCK + positive_offset[ids]
    partial, positive = None, 0.0
    for index in range(2):
        masks = jnp.arange(index * half, (index + 1) * half, dtype=jnp.int32)
        owner = (dp * n_cent + (cent ^ masks)) * rows
        column = (owner[:, None] + jnp.arange(rows, dtype=jnp.int32)[None, :]).reshape(-1)
        scores = SCALE * lax.dot_general(
            asked, held[index], (((1,), (1,)), ((), ())), preferred_element_type=jnp.float32
        )
        allowed = jnp.any(picks[:, :, None] == (column // BLOCK)[None, None, :], axis=1)
        top = jnp.max(jnp.where(allowed, scores, FAR), axis=1)
        total = jnp.sum(jnp.where(allowed, jnp.exp(scores - top[:, None]), 0.0), axis=1)
        losses.append((top, total))
        positive = positive + jnp.sum(jnp.where(column[None, :] == target[:, None], scores, 0.0), axis=1)
    top = jnp.maximum(losses[0][0], losses[1][0])
    total = sum(t * jnp.exp(m - top) for m, t in losses)
    found = jnp.stack([jnp.where(total > 0.0, top + jnp.log(jnp.maximum(total, 1e-37)), FAR), positive])
    for bit in dp_bits:
        other = swap(found, "dp", bit)
        found = jnp.stack([join_lse(found[0], other[0]), found[1] + other[1]])
    whole = found[0] - found[1]
    loss = lax.dynamic_slice_in_dim(whole, dp * own_queries, own_queries, 0)
    return means, loss


def solution(mesh):
    placed = (P(("dp", "cent"), None), P(("dp", "cent"), None), P("cent", None), P(), P())
    return jax.shard_map(
        on_device,
        mesh=mesh,
        in_specs=placed,
        out_specs=(P("cent", None), P(("dp", "cent"))),
        check_vma=False,
    )
```

```python
import jax
import jax.numpy as jnp
from jax import lax
from jax.sharding import PartitionSpec as P

BLOCK = 128
ITERS = 2
SHARPNESS = 0.05
SCALE = 0.05
PRIOR = 1.0
FAR = -1e30


def swap(value, axis, bit):
    size = lax.axis_size(axis)
    return lax.ppermute(value, axis, [(i, i ^ bit) for i in range(size)])


def bits_of(size):
    return [1 << k for k in range(size.bit_length() - 1)]


def in_order(mine, other, flag):
    return jnp.concatenate([jnp.where(flag == 0, mine, other), jnp.where(flag == 0, other, mine)])


def gathered_pieces(value, later, axis, size):
    far = size // 2
    half = value.shape[0] // 2
    pieces = {0: later}
    for mask in sorted(range(1, size), key=lambda m: (bin(m).count("1"), -m)):
        low = mask & -mask
        rest = mask ^ low
        if rest & (rest - 1):
            second = rest & -rest
            pieces[mask] = jnp.concatenate(
                [swap(pieces[rest][:half], axis, low), swap(pieces[mask ^ second][half:], axis, second)]
            )
        else:
            pieces[mask] = swap(value if mask == far else pieces[rest], axis, low)
    return pieces


def in_three(value):
    parts = []
    for _ in range(3):
        top = lax.reduce_precision(value, 8, 7)
        parts.append(top.astype(jnp.bfloat16))
        value = value - top
    return parts


def join_lse(first, second):
    top = jnp.maximum(first, second)
    return top + jnp.log(1.0 + jnp.exp(jnp.minimum(first, second) - top))


def on_device(passages, queries, init_centroids, pattern, positive_offset):
    n_dp, n_cent = lax.axis_size("dp"), lax.axis_size("cent")
    dp, cent = lax.axis_index("dp"), lax.axis_index("cent")
    dp_bits, cent_bits = bits_of(n_dp), bits_of(n_cent)
    core = dp & 1
    rows, width = passages.shape
    own_queries = queries.shape[0]
    half = n_cent // 2

    asked = swap(queries, "dp", dp_bits[0])
    asked, later = lax.optimization_barrier((asked, passages))

    pieces = gathered_pieces(passages, later, "cent", n_cent)
    pieces[1], means = lax.optimization_barrier((pieces[1], init_centroids))
    near = jnp.concatenate([pieces[mask] for mask in range(half)])
    far = jnp.concatenate([pieces[mask] for mask in range(half, n_cent)])
    held = [near, far]

    def loss_partials(asked, pattern, positive_offset, dp, cent):
        mine = (n_dp, n_cent, own_queries)
        picks = lax.dynamic_index_in_dim(pattern.reshape(mine + (-1,)), cent, 1, keepdims=False)
        picks = picks.reshape(n_dp * own_queries, -1)
        offset = lax.dynamic_index_in_dim(positive_offset.reshape(mine), cent, 1, keepdims=False).reshape(-1)
        target = picks[:, 0] * BLOCK + offset
        partials, positive = [], 0.0
        for index, group in enumerate(held):
            masks = jnp.arange(index * half, (index + 1) * half, dtype=jnp.int32)
            owner = (dp * n_cent + (cent ^ masks)) * rows
            column = (owner[:, None] + jnp.arange(rows, dtype=jnp.int32)[None, :]).reshape(-1)
            scores = SCALE * lax.dot_general(
                asked, group, (((1,), (1,)), ((), ())), preferred_element_type=jnp.float32
            )
            allowed = jnp.any(picks[:, :, None] == (column // BLOCK)[None, None, :], axis=1)
            top = jnp.max(jnp.where(allowed, scores, FAR), axis=1)
            total = jnp.sum(jnp.where(allowed, jnp.exp(scores - top[:, None]), 0.0), axis=1)
            partials.append(jnp.where(total > 0.0, top + jnp.log(jnp.maximum(total, 1e-37)), FAR))
            positive = positive + jnp.sum(jnp.where(column[None, :] == target[:, None], scores, 0.0), axis=1)
        return positive, join_lse(*partials)

    centers = means.shape[0]
    kept = centers // 2
    first = core == 0
    asks = n_dp * own_queries
    for step in range(ITERS):
        last = step == ITERS - 1
        centers_half = means.astype(jnp.bfloat16)
        norms = jnp.sum(means * means, axis=1)
        odds, stats = [], []
        for group in held:
            logits = SHARPNESS * (
                2.0
                * lax.dot_general(
                    centers_half, group, (((1,), (1,)), ((), ())), preferred_element_type=jnp.float32
                )
                - norms[:, None]
            )
            top = jnp.max(logits, axis=0)
            odds.append(logits)
            stats.append(top + jnp.log(jnp.sum(jnp.exp(logits - top[None, :]), axis=0)))
        lse = jnp.concatenate(stats).reshape((2,) * len(cent_bits) + (rows,))
        for bit in cent_bits:
            position = len(cent_bits) - 1 - cent_bits.index(bit)
            lse = join_lse(lse, jnp.flip(swap(lse, "cent", bit), axis=position))
            if last and bit == cent_bits[0]:
                inputs = (lse, asked, pattern, positive_offset, dp, cent)
                lse, *inputs = lax.optimization_barrier(inputs)
                positive, found = loss_partials(*inputs)
        lse = lse.reshape(2, half * rows)
        resps, counts = [], 0.0
        for index in range(2):
            resp = jnp.exp(odds[index] - lse[index][None, :])
            counts = counts + jnp.sum(resp, axis=1)
            resps.append(resp.astype(jnp.bfloat16))

        if step == 0:
            asked = in_order(queries, asked, core)
        line = jnp.where(first, counts[:kept], counts[kept:])
        rest = jnp.where(first, counts[kept:], counts[:kept])
        if last:
            line = jnp.concatenate([line, positive, found])
            rest = jnp.concatenate([rest, positive, found])

        def join_lines(line, other):
            cut = kept + asks
            if not last:
                return line + other
            return jnp.concatenate([line[:cut] + other[:cut], join_lse(line[cut:], other[cut:])])

        cut = width // 2
        totals = []
        for part in range(2):
            numer = 0.0
            for index in range(2):
                numer = numer + jnp.dot(
                    resps[index], held[index][:, part * cut : (part + 1) * cut], preferred_element_type=jnp.float32
                )
            if part == 0:
                numer, resps = lax.optimization_barrier((numer, resps))
            total = jnp.where(first, numer[:kept], numer[kept:])
            sent = jnp.where(first, numer[kept:], numer[:kept])
            if part == 0:
                sent = jnp.concatenate([sent, jnp.pad(rest[None, :], ((0, 7), (0, cut - rest.shape[0])))])
            other = swap(sent, "dp", dp_bits[0])
            totals.append(total + other[:kept])
            if part == 0:
                line = join_lines(line, other[kept, : line.shape[0]])
        for bit in dp_bits[1:]:
            for part in range(2):
                sent = totals[part].astype(jnp.bfloat16)
                packed = sent
                if part == 0:
                    parts = [jnp.pad(p[None, :], ((0, 0), (0, cut - p.shape[0]))) for p in in_three(line)]
                    packed = jnp.concatenate([packed] + parts)
                    if step == 0:
                        packed = jnp.concatenate([packed, asked[:, :cut], asked[:, cut:]])
                    packed = jnp.pad(packed, ((0, -packed.shape[0] % 8), (0, 0)))
                other = swap(packed, "dp", bit)
                totals[part] = sent.astype(jnp.float32) + other[:kept].astype(jnp.float32)
                if part == 0:
                    three = other[kept : kept + 3, : line.shape[0]].astype(jnp.float32)
                    line = join_lines(line, (three[0] + three[1]) + three[2])
                    if step == 0:
                        more = other[kept + 3 : kept + 3 + 2 * asked.shape[0]]
                        more = jnp.concatenate([more[: asked.shape[0]], more[asked.shape[0] :]], axis=1)
                        asked = in_order(asked, more, dp & bit)
        if last:
            whole = line[kept + asks :] - line[kept : kept + asks]
            loss = lax.dynamic_slice_in_dim(whole, dp * own_queries, own_queries, 0)
        prior = jnp.where(first, means[:kept], means[kept:])
        fresh = []
        for part in range(2):
            mine = (totals[part] + PRIOR * prior[:, part * cut : (part + 1) * cut]) / (line[:kept, None] + PRIOR)
            fresh.append(in_order(mine, swap(mine, "dp", dp_bits[0]), core))
        means = jnp.concatenate(fresh, axis=1)
    return means, loss


def solution(mesh):
    placed = (P(("dp", "cent"), None), P(("dp", "cent"), None), P("cent", None), P(), P())
    return jax.shard_map(
        on_device,
        mesh=mesh,
        in_specs=placed,
        out_specs=(P("cent", None), P(("dp", "cent"))),
        check_vma=False,
    )
```

```python
import jax
import jax.numpy as jnp
from jax import lax
from jax.sharding import PartitionSpec as P

BLOCK = 128
ITERS = 2
SHARPNESS = 0.05
SCALE = 0.05
PRIOR = 1.0
FAR = -1e30


def swap(value, axis, bit):
    size = lax.axis_size(axis)
    return lax.ppermute(value, axis, [(i, i ^ bit) for i in range(size)])


def bits_of(size):
    return [1 << k for k in range(size.bit_length() - 1)]


def in_order(mine, other, flag):
    return jnp.concatenate([jnp.where(flag == 0, mine, other), jnp.where(flag == 0, other, mine)])


def gathered_pieces(value, later, axis, size):
    far = size // 2
    half = 1 * value.shape[0] // 4
    pieces = {0: later}
    for mask in sorted(range(1, size), key=lambda m: (bin(m).count("1"), -m)):
        low = mask & -mask
        rest = mask ^ low
        if rest == far and mask == far + far // 2 and far > 1:
            later_far, pieces[far // 2] = lax.optimization_barrier((pieces[far], pieces[far // 2]))
            pieces[mask] = swap(later_far, axis, low)
            continue
        if rest & (rest - 1):
            second = rest & -rest
            pieces[mask] = jnp.concatenate(
                [swap(pieces[rest][:half], axis, low), swap(pieces[mask ^ second][half:], axis, second)]
            )
        else:
            pieces[mask] = swap(value if mask == far else pieces[rest], axis, low)
    return pieces


def in_three(value):
    parts = []
    for _ in range(3):
        top = lax.reduce_precision(value, 8, 7)
        parts.append(top.astype(jnp.bfloat16))
        value = value - top
    return parts


def join_lse(first, second):
    top = jnp.maximum(first, second)
    return top + jnp.log(1.0 + jnp.exp(jnp.minimum(first, second) - top))


def on_device(passages, queries, init_centroids, pattern, positive_offset):
    n_dp, n_cent = lax.axis_size("dp"), lax.axis_size("cent")
    dp, cent = lax.axis_index("dp"), lax.axis_index("cent")
    dp_bits, cent_bits = bits_of(n_dp), bits_of(n_cent)
    core = dp & 1
    rows, width = passages.shape
    own_queries = queries.shape[0]
    half = n_cent // 2

    asked = swap(queries, "dp", dp_bits[0])
    asked, later = lax.optimization_barrier((asked, passages))

    pieces = gathered_pieces(passages, later, "cent", n_cent)
    pieces[1], means = lax.optimization_barrier((pieces[1], init_centroids))
    near = jnp.concatenate([pieces[mask] for mask in range(half)])
    far = jnp.concatenate([pieces[mask] for mask in range(half, n_cent)])
    held = [near, far]

    def loss_partials(asked, pattern, positive_offset, dp, cent):
        mine = (n_dp, n_cent, own_queries)
        picks = lax.dynamic_index_in_dim(pattern.reshape(mine + (-1,)), cent, 1, keepdims=False)
        picks = picks.reshape(n_dp * own_queries, -1)
        offset = lax.dynamic_index_in_dim(positive_offset.reshape(mine), cent, 1, keepdims=False).reshape(-1)
        target = picks[:, 0] * BLOCK + offset
        partials, positive = [], 0.0
        for index, group in enumerate(held):
            masks = jnp.arange(index * half, (index + 1) * half, dtype=jnp.int32)
            owner = (dp * n_cent + (cent ^ masks)) * rows
            column = (owner[:, None] + jnp.arange(rows, dtype=jnp.int32)[None, :]).reshape(-1)
            scores = SCALE * lax.dot_general(
                asked, group, (((1,), (1,)), ((), ())), preferred_element_type=jnp.float32
            )
            allowed = jnp.any(picks[:, :, None] == (column // BLOCK)[None, None, :], axis=1)
            top = jnp.max(jnp.where(allowed, scores, FAR), axis=1)
            total = jnp.sum(jnp.where(allowed, jnp.exp(scores - top[:, None]), 0.0), axis=1)
            partials.append(jnp.where(total > 0.0, top + jnp.log(jnp.maximum(total, 1e-37)), FAR))
            positive = positive + jnp.sum(jnp.where(column[None, :] == target[:, None], scores, 0.0), axis=1)
        return positive, join_lse(*partials)

    centers = means.shape[0]
    kept = centers // 2
    first = core == 0
    asks = n_dp * own_queries
    for step in range(ITERS):
        last = step == ITERS - 1
        centers_half = means.astype(jnp.bfloat16)
        norms = jnp.sum(means * means, axis=1)
        odds, stats = [], []
        for group in held:
            logits = SHARPNESS * (
                2.0
                * lax.dot_general(
                    centers_half, group, (((1,), (1,)), ((), ())), preferred_element_type=jnp.float32
                )
                - norms[:, None]
            )
            top = jnp.max(logits, axis=0)
            odds.append(logits)
            stats.append(top + jnp.log(jnp.sum(jnp.exp(logits - top[None, :]), axis=0)))
        lse = jnp.concatenate(stats).reshape((2,) * len(cent_bits) + (rows,))
        for bit in cent_bits:
            position = len(cent_bits) - 1 - cent_bits.index(bit)
            lse = join_lse(lse, jnp.flip(swap(lse, "cent", bit), axis=position))
            if last and bit == cent_bits[0]:
                inputs = (lse, asked, pattern, positive_offset, dp, cent)
                lse, *inputs = lax.optimization_barrier(inputs)
                positive, found = loss_partials(*inputs)
        lse = lse.reshape(2, half * rows)
        resps, counts = [], 0.0
        for index in range(2):
            resp = jnp.exp(odds[index] - lse[index][None, :])
            counts = counts + jnp.sum(resp, axis=1)
            resps.append(resp.astype(jnp.bfloat16))

        if step == 0:
            asked = in_order(queries, asked, core)
        line = jnp.where(first, counts[:kept], counts[kept:])
        rest = jnp.where(first, counts[kept:], counts[:kept])
        if last:
            line = jnp.concatenate([line, positive, found])
            rest = jnp.concatenate([rest, positive, found])

        def join_lines(line, other):
            cut = kept + asks
            if not last:
                return line + other
            return jnp.concatenate([line[:cut] + other[:cut], join_lse(line[cut:], other[cut:])])

        cut = width // 2
        totals = []
        for part in range(2):
            numer = 0.0
            for index in range(2):
                numer = numer + jnp.dot(
                    resps[index], held[index][:, part * cut : (part + 1) * cut], preferred_element_type=jnp.float32
                )
            if part == 0:
                numer, resps = lax.optimization_barrier((numer, resps))
            total = jnp.where(first, numer[:kept], numer[kept:])
            sent = jnp.where(first, numer[kept:], numer[:kept])
            if part == 0:
                sent = jnp.concatenate([sent, jnp.pad(rest[None, :], ((0, 7), (0, cut - rest.shape[0])))])
            other = swap(sent, "dp", dp_bits[0])
            totals.append(total + other[:kept])
            if part == 0:
                line = join_lines(line, other[kept, : line.shape[0]])
        for bit in dp_bits[1:]:
            for part in range(2):
                sent = totals[part].astype(jnp.bfloat16)
                packed = sent
                if part == 0:
                    parts = jnp.pad(jnp.stack(in_three(line)), ((0, 5), (0, cut - line.shape[0])))
                    packed = jnp.concatenate([packed, parts])
                    if step == 0:
                        packed = jnp.concatenate([packed, asked[:, :cut], asked[:, cut:]])
                    packed = jnp.pad(packed, ((0, -packed.shape[0] % 8), (0, 0)))
                other = swap(packed, "dp", bit)
                totals[part] = sent.astype(jnp.float32) + other[:kept].astype(jnp.float32)
                if part == 0:
                    three = other[kept : kept + 3, : line.shape[0]].astype(jnp.float32)
                    line = join_lines(line, (three[0] + three[1]) + three[2])
                    if step == 0:
                        more = other[kept + 8 : kept + 8 + 2 * asked.shape[0]]
                        more = jnp.concatenate([more[: asked.shape[0]], more[asked.shape[0] :]], axis=1)
                        asked = in_order(asked, more, dp & bit)
        if last:
            whole = line[kept + asks :] - line[kept : kept + asks]
            loss = lax.dynamic_slice_in_dim(whole, dp * own_queries, own_queries, 0)
        prior = jnp.where(first, means[:kept], means[kept:])
        fresh = []
        for part in range(2):
            mine = (totals[part] + PRIOR * prior[:, part * cut : (part + 1) * cut]) / (line[:kept, None] + PRIOR)
            fresh.append(in_order(mine, swap(mine, "dp", dp_bits[0]), core))
        means = jnp.concatenate(fresh, axis=1)
    return means, loss


def solution(mesh):
    placed = (P(("dp", "cent"), None), P(("dp", "cent"), None), P("cent", None), P(), P())
    return jax.shard_map(
        on_device,
        mesh=mesh,
        in_specs=placed,
        out_specs=(P("cent", None), P(("dp", "cent"))),
        check_vma=False,
    )
```

```python
import jax
import jax.numpy as jnp
from jax import lax
from jax.sharding import PartitionSpec as P

BLOCK = 128
ITERS = 2
SHARPNESS = 0.05
SCALE = 0.05
PRIOR = 1.0
FAR = -1e30


def swap(value, axis, bit):
    size = lax.axis_size(axis)
    return lax.ppermute(value, axis, [(i, i ^ bit) for i in range(size)])


def bits_of(size):
    return [1 << k for k in range(size.bit_length() - 1)]


def in_order(mine, other, flag):
    return jnp.concatenate([jnp.where(flag == 0, mine, other), jnp.where(flag == 0, other, mine)])


def gathered_pieces(value, later, axis, size):
    far = size // 2
    half = 1 * value.shape[0] // 4
    pieces = {0: later}
    for mask in sorted(range(1, size), key=lambda m: (bin(m).count("1"), -m)):
        low = mask & -mask
        rest = mask ^ low
        if rest == far and mask == far + far // 2 and far > 1:
            later_far, pieces[far // 2] = lax.optimization_barrier((pieces[far], pieces[far // 2]))
            pieces[mask] = swap(later_far, axis, low)
            continue
        if rest & (rest - 1):
            second = rest & -rest
            pieces[mask] = jnp.concatenate(
                [swap(pieces[rest][:half], axis, low), swap(pieces[mask ^ second][half:], axis, second)]
            )
        else:
            pieces[mask] = swap(value if mask == far else pieces[rest], axis, low)
    return pieces


def in_three(value):
    parts = []
    for _ in range(3):
        top = lax.reduce_precision(value, 8, 7)
        parts.append(top.astype(jnp.bfloat16))
        value = value - top
    return parts


def join_lse(first, second):
    top = jnp.maximum(first, second)
    return top + jnp.log(1.0 + jnp.exp(jnp.minimum(first, second) - top))


def on_device(passages, queries, init_centroids, pattern, positive_offset):
    n_dp, n_cent = lax.axis_size("dp"), lax.axis_size("cent")
    dp, cent = lax.axis_index("dp"), lax.axis_index("cent")
    dp_bits, cent_bits = bits_of(n_dp), bits_of(n_cent)
    core = dp & 1
    rows, width = passages.shape
    own_queries = queries.shape[0]
    half = n_cent // 2

    asked = swap(queries, "dp", dp_bits[0])
    asked, later = lax.optimization_barrier((asked, passages))

    pieces = gathered_pieces(passages, later, "cent", n_cent)
    pieces[1], means = lax.optimization_barrier((pieces[1], init_centroids))
    near = jnp.concatenate([pieces[mask] for mask in range(half)])
    far = jnp.concatenate([pieces[mask] for mask in range(half, n_cent)])
    held = [near, far]

    def loss_partials(asked, pattern, positive_offset, dp, cent):
        mine = (n_dp, n_cent, own_queries)
        picks = lax.dynamic_index_in_dim(pattern.reshape(mine + (-1,)), cent, 1, keepdims=False)
        picks = picks.reshape(n_dp * own_queries, -1)
        offset = lax.dynamic_index_in_dim(positive_offset.reshape(mine), cent, 1, keepdims=False).reshape(-1)
        target = picks[:, 0] * BLOCK + offset
        partials, positive = [], 0.0
        for index, group in enumerate(held):
            masks = jnp.arange(index * half, (index + 1) * half, dtype=jnp.int32)
            owner = (dp * n_cent + (cent ^ masks)) * rows
            column = (owner[:, None] + jnp.arange(rows, dtype=jnp.int32)[None, :]).reshape(-1)
            scores = SCALE * lax.dot_general(
                asked, group, (((1,), (1,)), ((), ())), preferred_element_type=jnp.float32
            )
            allowed = jnp.any(picks[:, :, None] == (column // BLOCK)[None, None, :], axis=1)
            top = jnp.max(jnp.where(allowed, scores, FAR), axis=1)
            total = jnp.sum(jnp.where(allowed, jnp.exp(scores - top[:, None]), 0.0), axis=1)
            partials.append(jnp.where(total > 0.0, top + jnp.log(jnp.maximum(total, 1e-37)), FAR))
            positive = positive + jnp.sum(jnp.where(column[None, :] == target[:, None], scores, 0.0), axis=1)
        return positive, join_lse(*partials)

    centers = means.shape[0]
    kept = centers // 2
    first = core == 0
    asks = n_dp * own_queries
    for step in range(ITERS):
        last = step == ITERS - 1
        centers_half = means.astype(jnp.bfloat16)
        norms = jnp.sum(means * means, axis=1)
        odds, stats = [], []
        for group in held:
            logits = SHARPNESS * (
                2.0
                * lax.dot_general(
                    centers_half, group, (((1,), (1,)), ((), ())), preferred_element_type=jnp.float32
                )
                - norms[:, None]
            )
            top = jnp.max(logits, axis=0)
            odds.append(logits)
            stats.append(top + jnp.log(jnp.sum(jnp.exp(logits - top[None, :]), axis=0)))
        lse = jnp.concatenate(stats).reshape((2,) * len(cent_bits) + (rows,))
        for bit in cent_bits:
            position = len(cent_bits) - 1 - cent_bits.index(bit)
            lse = join_lse(lse, jnp.flip(swap(lse, "cent", bit), axis=position))
            if last and bit == cent_bits[0]:
                inputs = (lse, asked, pattern, positive_offset, dp, cent)
                lse, *inputs = lax.optimization_barrier(inputs)
                positive, found = loss_partials(*inputs)
        lse = lse.reshape(2, half * rows)
        resps, counts = [], 0.0
        for index in range(2):
            resp = jnp.exp(odds[index] - lse[index][None, :])
            counts = counts + jnp.sum(resp, axis=1)
            resps.append(resp.astype(jnp.bfloat16))

        if step == 0:
            asked = in_order(queries, asked, core)
        line = jnp.where(first, counts[:kept], counts[kept:])
        rest = jnp.where(first, counts[kept:], counts[:kept])
        if last:
            line = jnp.concatenate([line, positive, found])
            rest = jnp.concatenate([rest, positive, found])

        def join_lines(line, other):
            cut = kept + asks
            if not last:
                return line + other
            return jnp.concatenate([line[:cut] + other[:cut], join_lse(line[cut:], other[cut:])])

        cut = width // 2
        totals = []
        for part in range(2):
            numer = 0.0
            for index in range(2):
                numer = numer + jnp.dot(
                    resps[index], held[index][:, part * cut : (part + 1) * cut], preferred_element_type=jnp.float32
                )
            if part == 0:
                numer, resps = lax.optimization_barrier((numer, resps))
            total = jnp.where(first, numer[:kept], numer[kept:])
            sent = jnp.where(first, numer[kept:], numer[:kept])
            if part == 0:
                sent = jnp.concatenate([sent, jnp.pad(rest[None, :], ((0, 7), (0, cut - rest.shape[0])))])
            other = swap(sent, "dp", dp_bits[0])
            totals.append(total + other[:kept])
            if part == 0:
                line = join_lines(line, other[kept, : line.shape[0]])
        for bit in dp_bits[1:]:
            for part in range(2):
                sent = totals[part]
                if isinstance(sent, tuple):
                    sent = sent[0].astype(jnp.float32) + sent[1].astype(jnp.float32)
                sent = sent.astype(jnp.bfloat16)
                packed = sent
                if part == 0:
                    parts = jnp.pad(jnp.stack(in_three(line)), ((0, 5), (0, cut - line.shape[0])))
                    packed = jnp.concatenate([packed, parts])
                    if step == 0:
                        packed = jnp.concatenate([packed, asked[:, :cut], asked[:, cut:]])
                    packed = jnp.pad(packed, ((0, -packed.shape[0] % 8), (0, 0)))
                other = swap(packed, "dp", bit)
                totals[part] = (sent, other[:kept])
                if part == 0:
                    three = other[kept : kept + 3, : line.shape[0]].astype(jnp.float32)
                    line = join_lines(line, (three[0] + three[1]) + three[2])
                    if step == 0:
                        more = other[kept + 8 : kept + 8 + 2 * asked.shape[0]]
                        more = jnp.concatenate([more[: asked.shape[0]], more[asked.shape[0] :]], axis=1)
                        asked = in_order(asked, more, dp & bit)
        if last:
            whole = line[kept + asks :] - line[kept : kept + asks]
            loss = lax.dynamic_slice_in_dim(whole, dp * own_queries, own_queries, 0)
        prior = jnp.where(first, means[:kept], means[kept:])
        fresh = []
        for part in range(2):
            mine = totals[part][0].astype(jnp.float32) + totals[part][1].astype(jnp.float32)
            mine = (mine + PRIOR * prior[:, part * cut : (part + 1) * cut]) / (line[:kept, None] + PRIOR)
            if part == 0:
                totals[1], _ = lax.optimization_barrier((totals[1], mine))
            fresh.append(in_order(mine, swap(mine, "dp", dp_bits[0]), core))
        means = jnp.concatenate(fresh, axis=1)
    return means, loss


def solution(mesh):
    placed = (P(("dp", "cent"), None), P(("dp", "cent"), None), P("cent", None), P(), P())
    return jax.shard_map(
        on_device,
        mesh=mesh,
        in_specs=placed,
        out_specs=(P("cent", None), P(("dp", "cent"))),
        check_vma=False,
    )
```

```python
import jax
import jax.numpy as jnp
from jax import lax
from jax.sharding import PartitionSpec as P

BLOCK = 128
ITERS = 2
SHARPNESS = 0.05
SCALE = 0.05
PRIOR = 1.0
FAR = -1e30


def swap(value, axis, bit):
    size = lax.axis_size(axis)
    return lax.ppermute(value, axis, [(i, i ^ bit) for i in range(size)])


def bits_of(size):
    return [1 << k for k in range(size.bit_length() - 1)]


def in_order(mine, other, flag):
    return jnp.concatenate([jnp.where(flag == 0, mine, other), jnp.where(flag == 0, other, mine)])


def column_pieces(value, later, axis, size):
    far = size // 2
    pieces = {0: later}
    for mask in sorted(range(2, size, 2), key=lambda m: (bin(m).count("1"), -m)):
        low = mask & -mask
        pieces[mask] = swap(value if mask == far else pieces[mask ^ low], axis, low)
    return pieces


def in_three(value):
    parts = []
    for _ in range(3):
        top = lax.reduce_precision(value, 8, 7)
        parts.append(top.astype(jnp.bfloat16))
        value = value - top
    return parts


def join_lse(first, second):
    top = jnp.maximum(first, second)
    return top + jnp.log(1.0 + jnp.exp(jnp.minimum(first, second) - top))


def on_device(passages, queries, init_centroids, pattern, positive_offset):
    n_dp, n_cent = lax.axis_size("dp"), lax.axis_size("cent")
    dp, cent = lax.axis_index("dp"), lax.axis_index("cent")
    dp_bits, cent_bits = bits_of(n_dp), bits_of(n_cent)
    core = dp & 1
    rows, width = passages.shape
    own_queries = queries.shape[0]
    half = n_cent // 2

    asked = swap(queries, "dp", dp_bits[0])
    asked, later, means = lax.optimization_barrier((asked, passages, init_centroids))

    evens = list(range(0, n_cent, 2))
    pieces = column_pieces(passages, later, "cent", n_cent)
    across = {mask: swap(pieces[mask], "cent", 1) for mask in evens[:-1]}
    pieces[2], pieces[0] = lax.optimization_barrier((pieces[2], passages))
    held = [jnp.concatenate([pieces[mask] for mask in evens])]

    centers = means.shape[0]
    kept = centers // 2
    first = core == 0
    norms = jnp.sum(means * means, axis=1)
    centers_half = means.astype(jnp.bfloat16)
    packed = jnp.where(first, centers_half[:kept], centers_half[kept:])
    line = jnp.where(first, norms[:kept], norms[kept:])
    packed = jnp.concatenate([packed, jnp.pad(jnp.stack(in_three(line)), ((0, 5), (0, width - kept)))])
    mine = swap(packed, "cent", 1)
    other = swap(mine, "dp", dp_bits[0])
    partner_half = in_order(mine[:kept], other[:kept], core)
    lines = [part[kept : kept + 3, :kept].astype(jnp.float32) for part in (mine, other)]
    partner_norms = in_order(*[(three[0] + three[1]) + three[2] for three in lines], core)

    def loss_partials(asked, pattern, positive_offset, dp, cent):
        mine = (n_dp, n_cent, own_queries)
        picks = lax.dynamic_index_in_dim(pattern.reshape(mine + (-1,)), cent, 1, keepdims=False)
        picks = picks.reshape(n_dp * own_queries, -1)
        offset = lax.dynamic_index_in_dim(positive_offset.reshape(mine), cent, 1, keepdims=False).reshape(-1)
        target = picks[:, 0] * BLOCK + offset
        partials, positive = [], 0.0
        for index, group in enumerate(held):
            masks = jnp.array(evens, jnp.int32) | index
            owner = (dp * n_cent + (cent ^ masks)) * rows
            column = (owner[:, None] + jnp.arange(rows, dtype=jnp.int32)[None, :]).reshape(-1)
            scores = SCALE * lax.dot_general(
                asked, group, (((1,), (1,)), ((), ())), preferred_element_type=jnp.float32
            )
            allowed = jnp.any(picks[:, :, None] == (column // BLOCK)[None, None, :], axis=1)
            top = jnp.max(jnp.where(allowed, scores, FAR), axis=1)
            total = jnp.sum(jnp.where(allowed, jnp.exp(scores - top[:, None]), 0.0), axis=1)
            partials.append(jnp.where(total > 0.0, top + jnp.log(jnp.maximum(total, 1e-37)), FAR))
            positive = positive + jnp.sum(jnp.where(column[None, :] == target[:, None], scores, 0.0), axis=1)
        return positive, join_lse(*partials)

    def logits_of(centers_half, norms, group):
        products = lax.dot_general(centers_half, group, (((1,), (1,)), ((), ())), preferred_element_type=jnp.float32)
        return SHARPNESS * (2.0 * products - norms[:, None])

    def stats_of(*logits):
        top = jnp.max(logits[0], axis=0)
        for more in logits[1:]:
            top = jnp.maximum(top, jnp.max(more, axis=0))
        return top + jnp.log(sum(jnp.sum(jnp.exp(part - top[None, :]), axis=0) for part in logits))

    def over_column(bit, lse):
        axis = 0 if bit == 1 else len(cent_bits) - cent_bits.index(bit)
        return join_lse(lse, jnp.flip(swap(lse, "cent", bit), axis=axis))

    asks = n_dp * own_queries
    for step in range(ITERS):
        last = step == ITERS - 1
        shape = (-1,) + (2,) * (len(cent_bits) - 1) + (rows,)
        if step == 0:
            odds = [logits_of(centers_half, norms, held[0])]
            lse = stats_of(odds[0], logits_of(partner_half, partner_norms, held[0])).reshape(shape)
            lse, tail = lax.optimization_barrier((lse, pieces[evens[-1]]))
            across[evens[-1]] = swap(tail, "cent", 1)
            stops = [0, half // 4, half - half // 4, half]
            for index, bit in enumerate(cent_bits[1:] + [None]):
                ties = evens[stops[index] : stops[index + 1]] if index < 3 else []
                lse, *parts = lax.optimization_barrier([lse] + [across[mask] for mask in ties])
                across.update(zip(ties, parts))
                if bit is not None:
                    lse = over_column(bit, lse)
            held.append(jnp.concatenate([across[mask] for mask in evens]))
            lse = jnp.concatenate([lse, swap(lse, "cent", 1)])
            odds.append(logits_of(centers_half, norms, held[-1]))
            lse, odds[-1] = lax.optimization_barrier((lse, odds[-1]))
        else:
            norms = jnp.sum(means * means, axis=1)
            centers_half = means.astype(jnp.bfloat16)
            odds = [logits_of(centers_half, norms, group) for group in held]
            lse = jnp.concatenate([stats_of(part) for part in odds]).reshape(shape)
            for bit in cent_bits:
                lse = over_column(bit, lse)
                if last and bit == cent_bits[0]:
                    inputs = (lse, asked, pattern, positive_offset, dp, cent)
                    lse, *inputs = lax.optimization_barrier(inputs)
                    positive, found = loss_partials(*inputs)
        lse = lse.reshape(2, half * rows)
        resps, counts = [], 0.0
        for index in range(2):
            resp = jnp.exp(odds[index] - lse[index][None, :])
            counts = counts + jnp.sum(resp, axis=1)
            resps.append(resp.astype(jnp.bfloat16))

        if step == 0:
            asked = in_order(queries, asked, core)
        line = jnp.where(first, counts[:kept], counts[kept:])
        rest = jnp.where(first, counts[kept:], counts[:kept])
        if last:
            line = jnp.concatenate([line, positive, found])
            rest = jnp.concatenate([rest, positive, found])

        def join_lines(line, other):
            cut = kept + asks
            if not last:
                return line + other
            return jnp.concatenate([line[:cut] + other[:cut], join_lse(line[cut:], other[cut:])])

        cut = width // 2
        totals = []
        for part in range(2):
            numer = 0.0
            for index in range(2):
                numer = numer + jnp.dot(
                    resps[index], held[index][:, part * cut : (part + 1) * cut], preferred_element_type=jnp.float32
                )
            total = jnp.where(first, numer[:kept], numer[kept:])
            sent = jnp.where(first, numer[kept:], numer[:kept])
            if part == 0:
                sent = jnp.concatenate([sent, jnp.pad(rest[None, :], ((0, 7), (0, cut - rest.shape[0])))])
            if part == 0:
                resps, _ = lax.optimization_barrier((resps, sent))
            other = swap(sent, "dp", dp_bits[0])
            totals.append(total + other[:kept])
            if part == 0:
                line = join_lines(line, other[kept, : line.shape[0]])
        for bit in dp_bits[1:]:
            for part in range(2):
                sent = totals[part]
                if isinstance(sent, tuple):
                    sent = sent[0].astype(jnp.float32) + sent[1].astype(jnp.float32)
                sent = sent.astype(jnp.bfloat16)
                packed = sent
                if part == 0:
                    parts = jnp.pad(jnp.stack(in_three(line)), ((0, 5), (0, cut - line.shape[0])))
                    packed = jnp.concatenate([packed, parts])
                    if step == 0:
                        packed = jnp.concatenate([packed, asked[:, :cut], asked[:, cut:]])
                    packed = jnp.pad(packed, ((0, -packed.shape[0] % 8), (0, 0)))
                other = swap(packed, "dp", bit)
                totals[part] = (sent, other[:kept])
                if part == 0:
                    three = other[kept : kept + 3, : line.shape[0]].astype(jnp.float32)
                    line = join_lines(line, (three[0] + three[1]) + three[2])
                    if step == 0:
                        more = other[kept + 8 : kept + 8 + 2 * asked.shape[0]]
                        more = jnp.concatenate([more[: asked.shape[0]], more[asked.shape[0] :]], axis=1)
                        asked = in_order(asked, more, dp & bit)
        if last:
            whole = line[kept + asks :] - line[kept : kept + asks]
            loss = lax.dynamic_slice_in_dim(whole, dp * own_queries, own_queries, 0)
        prior = jnp.where(first, means[:kept], means[kept:])
        fresh = []
        for part in range(2):
            mine = totals[part][0].astype(jnp.float32) + totals[part][1].astype(jnp.float32)
            mine = (mine + PRIOR * prior[:, part * cut : (part + 1) * cut]) / (line[:kept, None] + PRIOR)
            if part == 0:
                totals[1], _ = lax.optimization_barrier((totals[1], mine))
            fresh.append(in_order(mine, swap(mine, "dp", dp_bits[0]), core))
        means = jnp.concatenate(fresh, axis=1)
    return means, loss


def solution(mesh):
    placed = (P(("dp", "cent"), None), P(("dp", "cent"), None), P("cent", None), P(), P())
    return jax.shard_map(
        on_device,
        mesh=mesh,
        in_specs=placed,
        out_specs=(P("cent", None), P(("dp", "cent"))),
        check_vma=False,
    )
```

```python
import jax
import jax.numpy as jnp
from jax import lax
from jax.sharding import PartitionSpec as P

BLOCK = 128
ITERS = 2
SHARPNESS = 0.05
SCALE = 0.05
PRIOR = 1.0
FAR = -1e30


def swap(value, axis, bit):
    size = lax.axis_size(axis)
    return lax.ppermute(value, axis, [(i, i ^ bit) for i in range(size)])


def bits_of(size):
    return [1 << k for k in range(size.bit_length() - 1)]


def in_order(mine, other, flag):
    return jnp.concatenate([jnp.where(flag == 0, mine, other), jnp.where(flag == 0, other, mine)])


def column_pieces(value, later, axis, size):
    far = size // 2
    pieces = {0: later}
    for mask in sorted(range(2, size, 2), key=lambda m: (bin(m).count("1"), -m)):
        low = mask & -mask
        pieces[mask] = swap(value if mask == far else pieces[mask ^ low], axis, low)
    return pieces


def in_three(value):
    parts = []
    for _ in range(3):
        top = lax.reduce_precision(value, 8, 7)
        parts.append(top.astype(jnp.bfloat16))
        value = value - top
    return parts


def join_lse(first, second):
    top = jnp.maximum(first, second)
    return top + jnp.log(1.0 + jnp.exp(jnp.minimum(first, second) - top))


def on_device(passages, queries, init_centroids, pattern, positive_offset):
    n_dp, n_cent = lax.axis_size("dp"), lax.axis_size("cent")
    dp, cent = lax.axis_index("dp"), lax.axis_index("cent")
    dp_bits, cent_bits = bits_of(n_dp), bits_of(n_cent)
    core = dp & 1
    rows, width = passages.shape
    own_queries = queries.shape[0]
    half = n_cent // 2

    asked = swap(queries, "dp", dp_bits[0])
    asked, later, means = lax.optimization_barrier((asked, passages, init_centroids))

    evens = list(range(0, n_cent, 2))
    pieces = column_pieces(passages, later, "cent", n_cent)
    across = {mask: swap(pieces[mask], "cent", 1) for mask in evens[:-1]}
    pieces[2], pieces[0] = lax.optimization_barrier((pieces[2], passages))
    held = [jnp.concatenate([pieces[mask] for mask in evens])]

    centers = means.shape[0]
    kept = centers // 2
    first = core == 0
    norms = jnp.sum(means * means, axis=1)
    centers_half = means.astype(jnp.bfloat16)
    packed = jnp.where(first, centers_half[:kept], centers_half[kept:])
    line = jnp.where(first, norms[:kept], norms[kept:])
    packed = jnp.concatenate([packed, jnp.pad(jnp.stack(in_three(line)), ((0, 5), (0, width - kept)))])
    mine = swap(packed, "cent", 1)
    other = swap(mine, "dp", dp_bits[0])
    partner_half = in_order(mine[:kept], other[:kept], core)
    lines = [part[kept : kept + 3, :kept].astype(jnp.float32) for part in (mine, other)]
    partner_norms = in_order(*[(three[0] + three[1]) + three[2] for three in lines], core)

    def loss_partials(asked, pattern, positive_offset, dp, cent):
        mine = (n_dp, n_cent, own_queries)
        picks = lax.dynamic_index_in_dim(pattern.reshape(mine + (-1,)), cent, 1, keepdims=False)
        picks = picks.reshape(n_dp * own_queries, -1)
        offset = lax.dynamic_index_in_dim(positive_offset.reshape(mine), cent, 1, keepdims=False).reshape(-1)
        target = picks[:, 0] * BLOCK + offset
        partials, positive = [], 0.0
        for index, group in enumerate(held):
            masks = jnp.array(evens, jnp.int32) | index
            owner = (dp * n_cent + (cent ^ masks)) * rows
            column = (owner[:, None] + jnp.arange(rows, dtype=jnp.int32)[None, :]).reshape(-1)
            scores = SCALE * lax.dot_general(
                asked, group, (((1,), (1,)), ((), ())), preferred_element_type=jnp.float32
            )
            allowed = jnp.any(picks[:, :, None] == (column // BLOCK)[None, None, :], axis=1)
            top = jnp.max(jnp.where(allowed, scores, FAR), axis=1)
            total = jnp.sum(jnp.where(allowed, jnp.exp(scores - top[:, None]), 0.0), axis=1)
            partials.append(jnp.where(total > 0.0, top + jnp.log(jnp.maximum(total, 1e-37)), FAR))
            positive = positive + jnp.sum(jnp.where(column[None, :] == target[:, None], scores, 0.0), axis=1)
        return positive, join_lse(*partials)

    def logits_of(centers_half, norms, group):
        products = lax.dot_general(centers_half, group, (((1,), (1,)), ((), ())), preferred_element_type=jnp.float32)
        return SHARPNESS * (2.0 * products - norms[:, None])

    def stats_of(*logits):
        top = jnp.max(logits[0], axis=0)
        for more in logits[1:]:
            top = jnp.maximum(top, jnp.max(more, axis=0))
        return top + jnp.log(sum(jnp.sum(jnp.exp(part - top[None, :]), axis=0) for part in logits))

    def over_column(bit, lse):
        axis = 0 if bit == 1 else len(cent_bits) - cent_bits.index(bit)
        return join_lse(lse, jnp.flip(swap(lse, "cent", bit), axis=axis))

    asks = n_dp * own_queries
    for step in range(ITERS):
        last = step == ITERS - 1
        shape = (-1,) + (2,) * (len(cent_bits) - 1) + (rows,)
        if step == 0:
            odds = [logits_of(centers_half, norms, held[0])]
            lse = stats_of(odds[0], logits_of(partner_half, partner_norms, held[0])).reshape(shape)
            lse, held[0] = lax.optimization_barrier((lse, held[0]))
            across[evens[-1]] = swap(held[0][-rows:], "cent", 1)
            stops = [0, half // 4, half // 2, half]
            turn = evens
            for index, bit in enumerate(cent_bits[1:] + [None]):
                ties = turn[stops[index] : stops[index + 1]] if index < 3 else []
                lse, *parts = lax.optimization_barrier([lse] + [across[mask] for mask in ties])
                across.update(zip(ties, parts))
                if bit is not None:
                    lse = over_column(bit, lse)
            held.append(jnp.concatenate([across[mask] for mask in evens]))
            lse = jnp.concatenate([lse, swap(lse, "cent", 1)])
            odds.append(logits_of(centers_half, norms, held[-1]))
            lse, odds[-1] = lax.optimization_barrier((lse, odds[-1]))
        else:
            norms = jnp.sum(means * means, axis=1)
            centers_half = means.astype(jnp.bfloat16)
            odds = [logits_of(centers_half, norms, group) for group in held]
            lse = jnp.concatenate([stats_of(part) for part in odds]).reshape(shape)
            for bit in cent_bits:
                lse = over_column(bit, lse)
                if last and bit == cent_bits[0]:
                    inputs = (lse, asked, pattern, positive_offset, dp, cent)
                    lse, *inputs = lax.optimization_barrier(inputs)
                    positive, found = loss_partials(*inputs)
        lse = lse.reshape(2, half * rows)
        resps, counts = [], 0.0
        for index in range(2):
            resp = jnp.exp(odds[index] - lse[index][None, :])
            counts = counts + jnp.sum(resp, axis=1)
            resps.append(resp.astype(jnp.bfloat16))

        if step == 0:
            asked = in_order(queries, asked, core)
        line = jnp.where(first, counts[:kept], counts[kept:])
        rest = jnp.where(first, counts[kept:], counts[:kept])
        if last:
            line = jnp.concatenate([line, positive, found])
            rest = jnp.concatenate([rest, positive, found])

        def join_lines(line, other):
            cut = kept + asks
            if not last:
                return line + other
            return jnp.concatenate([line[:cut] + other[:cut], join_lse(line[cut:], other[cut:])])

        cut = width // 2
        totals = []
        for part in range(2):
            numer = 0.0
            for index in range(2):
                numer = numer + jnp.dot(
                    resps[index], held[index][:, part * cut : (part + 1) * cut], preferred_element_type=jnp.float32
                )
            total = jnp.where(first, numer[:kept], numer[kept:])
            sent = jnp.where(first, numer[kept:], numer[:kept])
            if part == 0:
                sent = jnp.concatenate([sent, jnp.pad(rest[None, :], ((0, 7), (0, cut - rest.shape[0])))])
            if part == 0:
                resps, _ = lax.optimization_barrier((resps, sent))
            other = swap(sent, "dp", dp_bits[0])
            totals.append(total + other[:kept])
            if part == 0:
                line = join_lines(line, other[kept, : line.shape[0]])
        for bit in dp_bits[1:]:
            for part in range(2):
                sent = totals[part]
                if isinstance(sent, tuple):
                    sent = sent[0].astype(jnp.float32) + sent[1].astype(jnp.float32)
                sent = sent.astype(jnp.bfloat16)
                packed = sent
                if part == 0:
                    parts = jnp.pad(jnp.stack(in_three(line)), ((0, 5), (0, cut - line.shape[0])))
                    packed = jnp.concatenate([packed, parts])
                    if step == 0:
                        packed = jnp.concatenate([packed, asked[:, :cut], asked[:, cut:]])
                    packed = jnp.pad(packed, ((0, -packed.shape[0] % 8), (0, 0)))
                other = swap(packed, "dp", bit)
                totals[part] = (sent, other[:kept])
                if part == 0:
                    three = other[kept : kept + 3, : line.shape[0]].astype(jnp.float32)
                    line = join_lines(line, (three[0] + three[1]) + three[2])
                    if step == 0:
                        more = other[kept + 8 : kept + 8 + 2 * asked.shape[0]]
                        more = jnp.concatenate([more[: asked.shape[0]], more[asked.shape[0] :]], axis=1)
                        asked = in_order(asked, more, dp & bit)
        if last:
            whole = line[kept + asks :] - line[kept : kept + asks]
            loss = lax.dynamic_slice_in_dim(whole, dp * own_queries, own_queries, 0)
        prior = jnp.where(first, means[:kept], means[kept:])
        fresh = []
        for part in range(2):
            mine = totals[part][0].astype(jnp.float32) + totals[part][1].astype(jnp.float32)
            mine = (mine + PRIOR * prior[:, part * cut : (part + 1) * cut]) / (line[:kept, None] + PRIOR)
            if part == 0:
                totals[1], _ = lax.optimization_barrier((totals[1], mine))
            fresh.append(in_order(mine, swap(mine, "dp", dp_bits[0]), core))
        means = jnp.concatenate(fresh, axis=1)
    return means, loss


def solution(mesh):
    placed = (P(("dp", "cent"), None), P(("dp", "cent"), None), P("cent", None), P(), P())
    return jax.shard_map(
        on_device,
        mesh=mesh,
        in_specs=placed,
        out_specs=(P("cent", None), P(("dp", "cent"))),
        check_vma=False,
    )
```

```python
import jax
import jax.numpy as jnp
from jax import lax
from jax.sharding import PartitionSpec as P

BLOCK = 128
ITERS = 2
SHARPNESS = 0.05
SCALE = 0.05
PRIOR = 1.0
FAR = -1e30


def swap(value, axis, bit):
    size = lax.axis_size(axis)
    return lax.ppermute(value, axis, [(i, i ^ bit) for i in range(size)])


def bits_of(size):
    return [1 << k for k in range(size.bit_length() - 1)]


def in_order(mine, other, flag):
    return jnp.concatenate([jnp.where(flag == 0, mine, other), jnp.where(flag == 0, other, mine)])


def column_pieces(value, later, axis, size):
    far = size // 2
    pieces = {0: later}
    for mask in sorted(range(2, size, 2), key=lambda m: (bin(m).count("1"), -m)):
        low = mask & -mask
        pieces[mask] = swap(value if mask == far else pieces[mask ^ low], axis, low)
    return pieces


def in_three(value):
    parts = []
    for _ in range(3):
        top = lax.reduce_precision(value, 8, 7)
        parts.append(top.astype(jnp.bfloat16))
        value = value - top
    return parts


def join_lse(first, second):
    top = jnp.maximum(first, second)
    return top + jnp.log(1.0 + jnp.exp(jnp.minimum(first, second) - top))


def on_device(passages, queries, init_centroids, pattern, positive_offset):
    n_dp, n_cent = lax.axis_size("dp"), lax.axis_size("cent")
    dp, cent = lax.axis_index("dp"), lax.axis_index("cent")
    dp_bits, cent_bits = bits_of(n_dp), bits_of(n_cent)
    core = dp & 1
    rows, width = passages.shape
    own_queries = queries.shape[0]
    half = n_cent // 2

    asked = swap(queries, "dp", dp_bits[0])
    asked, later, means = lax.optimization_barrier((asked, passages, init_centroids))

    evens = list(range(0, n_cent, 2))
    pieces = column_pieces(passages, later, "cent", n_cent)
    across = {mask: swap(pieces[mask], "cent", 1) for mask in evens[:-1]}
    asked = in_order(queries, asked, core)
    for bit in dp_bits[1:]:
        asked = in_order(asked, swap(asked, "dp", bit), dp & bit)
    pieces[2], pieces[0] = lax.optimization_barrier((pieces[2], passages))
    pieces[evens[-1]], asked = lax.optimization_barrier((pieces[evens[-1]], asked))
    held = [jnp.concatenate([pieces[mask] for mask in evens])]

    centers = means.shape[0]
    kept = centers // 2
    first = core == 0
    norms = jnp.sum(means * means, axis=1)
    centers_half = means.astype(jnp.bfloat16)
    packed = jnp.where(first, centers_half[:kept], centers_half[kept:])
    line = jnp.where(first, norms[:kept], norms[kept:])
    packed = jnp.concatenate([packed, jnp.pad(jnp.stack(in_three(line)), ((0, 5), (0, width - kept)))])
    mine = swap(packed, "cent", 1)
    other = swap(mine, "dp", dp_bits[0])
    partner_half = in_order(mine[:kept], other[:kept], core)
    lines = [part[kept : kept + 3, :kept].astype(jnp.float32) for part in (mine, other)]
    partner_norms = in_order(*[(three[0] + three[1]) + three[2] for three in lines], core)

    def loss_partials(asked, pattern, positive_offset, dp, cent):
        mine = (n_dp, n_cent, own_queries)
        picks = lax.dynamic_index_in_dim(pattern.reshape(mine + (-1,)), cent, 1, keepdims=False)
        picks = picks.reshape(n_dp * own_queries, -1)
        offset = lax.dynamic_index_in_dim(positive_offset.reshape(mine), cent, 1, keepdims=False).reshape(-1)
        target = picks[:, 0] * BLOCK + offset
        partials, positive = [], 0.0
        for index, group in enumerate(held):
            masks = jnp.array(evens, jnp.int32) | index
            owner = (dp * n_cent + (cent ^ masks)) * rows
            column = (owner[:, None] + jnp.arange(rows, dtype=jnp.int32)[None, :]).reshape(-1)
            scores = SCALE * lax.dot_general(
                asked, group, (((1,), (1,)), ((), ())), preferred_element_type=jnp.float32
            )
            allowed = jnp.any(picks[:, :, None] == (column // BLOCK)[None, None, :], axis=1)
            top = jnp.max(jnp.where(allowed, scores, FAR), axis=1)
            total = jnp.sum(jnp.where(allowed, jnp.exp(scores - top[:, None]), 0.0), axis=1)
            partials.append(jnp.where(total > 0.0, top + jnp.log(jnp.maximum(total, 1e-37)), FAR))
            positive = positive + jnp.sum(jnp.where(column[None, :] == target[:, None], scores, 0.0), axis=1)
        return positive, join_lse(*partials)

    def logits_of(centers_half, norms, group):
        products = lax.dot_general(centers_half, group, (((1,), (1,)), ((), ())), preferred_element_type=jnp.float32)
        return SHARPNESS * (2.0 * products - norms[:, None])

    def stats_of(*logits):
        top = jnp.max(logits[0], axis=0)
        for more in logits[1:]:
            top = jnp.maximum(top, jnp.max(more, axis=0))
        return top + jnp.log(sum(jnp.sum(jnp.exp(part - top[None, :]), axis=0) for part in logits))

    def over_column(bit, lse):
        axis = 0 if bit == 1 else len(cent_bits) - cent_bits.index(bit)
        return join_lse(lse, jnp.flip(swap(lse, "cent", bit), axis=axis))

    asks = n_dp * own_queries
    for step in range(ITERS):
        last = step == ITERS - 1
        shape = (-1,) + (2,) * (len(cent_bits) - 1) + (rows,)
        if step == 0:
            odds = [logits_of(centers_half, norms, held[0])]
            lse = stats_of(odds[0], logits_of(partner_half, partner_norms, held[0])).reshape(shape)
            lse, held[0] = lax.optimization_barrier((lse, held[0]))
            across[evens[-1]] = swap(held[0][-rows:], "cent", 1)
            stops = [0, half // 4, half // 2, half]
            turn = evens
            for index, bit in enumerate(cent_bits[1:] + [None]):
                ties = turn[stops[index] : stops[index + 1]] if index < 3 else []
                lse, *parts = lax.optimization_barrier([lse] + [across[mask] for mask in ties])
                across.update(zip(ties, parts))
                if bit is not None:
                    lse = over_column(bit, lse)
            held.append(jnp.concatenate([across[mask] for mask in evens]))
            lse = jnp.concatenate([lse, swap(lse, "cent", 1)])
            odds.append(logits_of(centers_half, norms, held[-1]))
            lse, odds[-1] = lax.optimization_barrier((lse, odds[-1]))
        else:
            norms = jnp.sum(means * means, axis=1)
            centers_half = means.astype(jnp.bfloat16)
            odds = [logits_of(centers_half, norms, group) for group in held]
            lse = jnp.concatenate([stats_of(part) for part in odds]).reshape(shape)
            for bit in cent_bits:
                lse = over_column(bit, lse)
                if last and bit == cent_bits[0]:
                    inputs = (lse, asked, pattern, positive_offset, dp, cent)
                    lse, *inputs = lax.optimization_barrier(inputs)
                    positive, found = loss_partials(*inputs)
        lse = lse.reshape(2, half * rows)
        resps, counts = [], 0.0
        for index in range(2):
            resp = jnp.exp(odds[index] - lse[index][None, :])
            counts = counts + jnp.sum(resp, axis=1)
            resps.append(resp.astype(jnp.bfloat16))

        line = jnp.where(first, counts[:kept], counts[kept:])
        rest = jnp.where(first, counts[kept:], counts[:kept])
        if last:
            line = jnp.concatenate([line, positive, found])
            rest = jnp.concatenate([rest, positive, found])

        def join_lines(line, other):
            cut = kept + asks
            if not last:
                return line + other
            return jnp.concatenate([line[:cut] + other[:cut], join_lse(line[cut:], other[cut:])])

        cut = width // 2
        totals = []
        for part in range(2):
            numer = 0.0
            for index in range(2):
                numer = numer + jnp.dot(
                    resps[index], held[index][:, part * cut : (part + 1) * cut], preferred_element_type=jnp.float32
                )
            total = jnp.where(first, numer[:kept], numer[kept:])
            sent = jnp.where(first, numer[kept:], numer[:kept])
            if part == 0:
                sent = jnp.concatenate([sent, jnp.pad(rest[None, :], ((0, 7), (0, cut - rest.shape[0])))])
            if part == 0:
                resps, _ = lax.optimization_barrier((resps, sent))
            other = swap(sent, "dp", dp_bits[0])
            totals.append(total + other[:kept])
            if part == 0:
                line = join_lines(line, other[kept, : line.shape[0]])
        for bit in dp_bits[1:]:
            for part in range(2):
                sent = totals[part]
                if isinstance(sent, tuple):
                    sent = sent[0].astype(jnp.float32) + sent[1].astype(jnp.float32)
                sent = sent.astype(jnp.bfloat16)
                packed = sent
                if part == 0:
                    parts = jnp.pad(jnp.stack(in_three(line)), ((0, 5), (0, cut - line.shape[0])))
                    packed = jnp.concatenate([packed, parts])
                    packed = jnp.pad(packed, ((0, -packed.shape[0] % 8), (0, 0)))
                other = swap(packed, "dp", bit)
                totals[part] = (sent, other[:kept])
                if part == 0:
                    three = other[kept : kept + 3, : line.shape[0]].astype(jnp.float32)
                    line = join_lines(line, (three[0] + three[1]) + three[2])
        if last:
            whole = line[kept + asks :] - line[kept : kept + asks]
            loss = lax.dynamic_slice_in_dim(whole, dp * own_queries, own_queries, 0)
        prior = jnp.where(first, means[:kept], means[kept:])
        fresh = []
        for part in range(2):
            mine = totals[part][0].astype(jnp.float32) + totals[part][1].astype(jnp.float32)
            mine = (mine + PRIOR * prior[:, part * cut : (part + 1) * cut]) / (line[:kept, None] + PRIOR)
            if part == 0:
                totals[1], _ = lax.optimization_barrier((totals[1], mine))
            fresh.append(in_order(mine, swap(mine, "dp", dp_bits[0]), core))
        means = jnp.concatenate(fresh, axis=1)
    return means, loss


def solution(mesh):
    placed = (P(("dp", "cent"), None), P(("dp", "cent"), None), P("cent", None), P(), P())
    return jax.shard_map(
        on_device,
        mesh=mesh,
        in_specs=placed,
        out_specs=(P("cent", None), P(("dp", "cent"))),
        check_vma=False,
    )
```

```python
import jax
import jax.numpy as jnp
from jax import lax
from jax.sharding import PartitionSpec as P

BLOCK = 128
ITERS = 2
SHARPNESS = 0.05
SCALE = 0.05
PRIOR = 1.0
FAR = -1e30


def swap(value, axis, bit):
    size = lax.axis_size(axis)
    return lax.ppermute(value, axis, [(i, i ^ bit) for i in range(size)])


def bits_of(size):
    return [1 << k for k in range(size.bit_length() - 1)]


def in_order(mine, other, flag):
    return jnp.concatenate([jnp.where(flag == 0, mine, other), jnp.where(flag == 0, other, mine)])


def column_pieces(value, later, axis, size):
    far = size // 2
    pieces = {0: later}
    for mask in sorted(range(2, size, 2), key=lambda m: (bin(m).count("1"), -m)):
        low = mask & -mask
        pieces[mask] = swap(value if mask == far else pieces[mask ^ low], axis, low)
    return pieces


def in_three(value):
    parts = []
    for _ in range(3):
        top = lax.reduce_precision(value, 8, 7)
        parts.append(top.astype(jnp.bfloat16))
        value = value - top
    return parts


def join_lse(first, second):
    top = jnp.maximum(first, second)
    return top + jnp.log(1.0 + jnp.exp(jnp.minimum(first, second) - top))


def on_device(passages, queries, init_centroids, pattern, positive_offset):
    n_dp, n_cent = lax.axis_size("dp"), lax.axis_size("cent")
    dp, cent = lax.axis_index("dp"), lax.axis_index("cent")
    dp_bits, cent_bits = bits_of(n_dp), bits_of(n_cent)
    core = dp & 1
    rows, width = passages.shape
    own_queries = queries.shape[0]
    half = n_cent // 2

    asked = swap(queries, "dp", dp_bits[0])
    asked, later, means = lax.optimization_barrier((asked, passages, init_centroids))

    evens = list(range(0, n_cent, 2))
    pieces = column_pieces(passages, later, "cent", n_cent)
    far = evens[half // 2]
    late, pieces[2] = lax.optimization_barrier((pieces[far], pieces[2]))
    across = {mask: swap(late if mask == far else pieces[mask], "cent", 1) for mask in evens[:-1]}
    asked = in_order(queries, asked, core)
    for bit in dp_bits[1:]:
        asked = in_order(asked, swap(asked, "dp", bit), dp & bit)
    pieces[2], pieces[0] = lax.optimization_barrier((pieces[2], passages))
    pieces[evens[-1]], asked = lax.optimization_barrier((pieces[evens[-1]], asked))
    held = [jnp.concatenate([pieces[mask] for mask in evens])]

    centers = means.shape[0]
    kept = centers // 2
    first = core == 0
    norms = jnp.sum(means * means, axis=1)
    centers_half = means.astype(jnp.bfloat16)
    packed = jnp.where(first, centers_half[:kept], centers_half[kept:])
    line = jnp.where(first, norms[:kept], norms[kept:])
    packed = jnp.concatenate([packed, jnp.pad(jnp.stack(in_three(line)), ((0, 5), (0, width - kept)))])
    mine = swap(packed, "cent", 1)
    other = swap(mine, "dp", dp_bits[0])
    partner_half = in_order(mine[:kept], other[:kept], core)
    lines = [part[kept : kept + 3, :kept].astype(jnp.float32) for part in (mine, other)]
    partner_norms = in_order(*[(three[0] + three[1]) + three[2] for three in lines], core)

    def loss_partials(asked, pattern, positive_offset, dp, cent):
        mine = (n_dp, n_cent, own_queries)
        picks = lax.dynamic_index_in_dim(pattern.reshape(mine + (-1,)), cent, 1, keepdims=False)
        picks = picks.reshape(n_dp * own_queries, -1)
        offset = lax.dynamic_index_in_dim(positive_offset.reshape(mine), cent, 1, keepdims=False).reshape(-1)
        target = picks[:, 0] * BLOCK + offset
        partials, positive = [], 0.0
        for index, group in enumerate(held):
            masks = jnp.array(evens, jnp.int32) | index
            owner = (dp * n_cent + (cent ^ masks)) * rows
            column = (owner[:, None] + jnp.arange(rows, dtype=jnp.int32)[None, :]).reshape(-1)
            scores = SCALE * lax.dot_general(
                asked, group, (((1,), (1,)), ((), ())), preferred_element_type=jnp.float32
            )
            allowed = jnp.any(picks[:, :, None] == (column // BLOCK)[None, None, :], axis=1)
            top = jnp.max(jnp.where(allowed, scores, FAR), axis=1)
            total = jnp.sum(jnp.where(allowed, jnp.exp(scores - top[:, None]), 0.0), axis=1)
            partials.append(jnp.where(total > 0.0, top + jnp.log(jnp.maximum(total, 1e-37)), FAR))
            positive = positive + jnp.sum(jnp.where(column[None, :] == target[:, None], scores, 0.0), axis=1)
        return positive, join_lse(*partials)

    def logits_of(centers_half, norms, group):
        products = lax.dot_general(centers_half, group, (((1,), (1,)), ((), ())), preferred_element_type=jnp.float32)
        return SHARPNESS * (2.0 * products - norms[:, None])

    def stats_of(*logits):
        top = jnp.max(logits[0], axis=0)
        for more in logits[1:]:
            top = jnp.maximum(top, jnp.max(more, axis=0))
        return top + jnp.log(sum(jnp.sum(jnp.exp(part - top[None, :]), axis=0) for part in logits))

    def over_column(bit, lse):
        axis = 0 if bit == 1 else len(cent_bits) - cent_bits.index(bit)
        return join_lse(lse, jnp.flip(swap(lse, "cent", bit), axis=axis))

    asks = n_dp * own_queries
    for step in range(ITERS):
        last = step == ITERS - 1
        shape = (-1,) + (2,) * (len(cent_bits) - 1) + (rows,)
        if step == 0:
            odds = [logits_of(centers_half, norms, held[0])]
            lse = stats_of(odds[0], logits_of(partner_half, partner_norms, held[0])).reshape(shape)
            lse, held[0] = lax.optimization_barrier((lse, held[0]))
            across[evens[-1]] = swap(held[0][-rows:], "cent", 1)
            stops = [0, half // 4, half // 2, half]
            turn = evens
            for index, bit in enumerate(cent_bits[1:] + [None]):
                ties = turn[stops[index] : stops[index + 1]] if index < 3 else []
                lse, *parts = lax.optimization_barrier([lse] + [across[mask] for mask in ties])
                across.update(zip(ties, parts))
                if bit is not None:
                    lse = over_column(bit, lse)
            held.append(jnp.concatenate([across[mask] for mask in evens]))
            lse = jnp.concatenate([lse, swap(lse, "cent", 1)])
            odds.append(logits_of(centers_half, norms, held[-1]))
            lse, odds[-1] = lax.optimization_barrier((lse, odds[-1]))
        else:
            norms = jnp.sum(means * means, axis=1)
            centers_half = means.astype(jnp.bfloat16)
            odds = [logits_of(centers_half, norms, group) for group in held]
            lse = jnp.concatenate([stats_of(part) for part in odds]).reshape(shape)
            for bit in cent_bits:
                lse = over_column(bit, lse)
                if last and bit == cent_bits[0]:
                    inputs = (lse, asked, pattern, positive_offset, dp, cent)
                    lse, *inputs = lax.optimization_barrier(inputs)
                    positive, found = loss_partials(*inputs)
        lse = lse.reshape(2, half * rows)
        resps, counts = [], 0.0
        for index in range(2):
            resp = jnp.exp(odds[index] - lse[index][None, :])
            counts = counts + jnp.sum(resp, axis=1)
            resps.append(resp.astype(jnp.bfloat16))

        line = jnp.where(first, counts[:kept], counts[kept:])
        rest = jnp.where(first, counts[kept:], counts[:kept])
        if last:
            line = jnp.concatenate([line, positive, found])
            rest = jnp.concatenate([rest, positive, found])

        def join_lines(line, other):
            cut = kept + asks
            if not last:
                return line + other
            return jnp.concatenate([line[:cut] + other[:cut], join_lse(line[cut:], other[cut:])])

        cut = width // 2
        totals = []
        for part in range(2):
            numer = 0.0
            for index in range(2):
                numer = numer + jnp.dot(
                    resps[index], held[index][:, part * cut : (part + 1) * cut], preferred_element_type=jnp.float32
                )
            total = jnp.where(first, numer[:kept], numer[kept:])
            sent = jnp.where(first, numer[kept:], numer[:kept])
            if part == 0:
                sent = jnp.concatenate([sent, jnp.pad(rest[None, :], ((0, 7), (0, cut - rest.shape[0])))])
            if part == 0:
                resps, _ = lax.optimization_barrier((resps, sent))
            other = swap(sent, "dp", dp_bits[0])
            totals.append(total + other[:kept])
            if part == 0:
                line = join_lines(line, other[kept, : line.shape[0]])
        for bit in dp_bits[1:]:
            for part in range(2):
                sent = totals[part]
                if isinstance(sent, tuple):
                    sent = sent[0].astype(jnp.float32) + sent[1].astype(jnp.float32)
                sent = sent.astype(jnp.bfloat16)
                packed = sent
                if part == 0:
                    parts = jnp.pad(jnp.stack(in_three(line)), ((0, 5), (0, cut - line.shape[0])))
                    packed = jnp.concatenate([packed, parts])
                    packed = jnp.pad(packed, ((0, -packed.shape[0] % 8), (0, 0)))
                other = swap(packed, "dp", bit)
                totals[part] = (sent, other[:kept])
                if part == 0:
                    three = other[kept : kept + 3, : line.shape[0]].astype(jnp.float32)
                    line = join_lines(line, (three[0] + three[1]) + three[2])
        if last:
            whole = line[kept + asks :] - line[kept : kept + asks]
            loss = lax.dynamic_slice_in_dim(whole, dp * own_queries, own_queries, 0)
        prior = jnp.where(first, means[:kept], means[kept:])
        fresh = []
        for part in range(2):
            mine = totals[part][0].astype(jnp.float32) + totals[part][1].astype(jnp.float32)
            mine = (mine + PRIOR * prior[:, part * cut : (part + 1) * cut]) / (line[:kept, None] + PRIOR)
            if part == 0:
                totals[1], _ = lax.optimization_barrier((totals[1], mine))
            fresh.append(in_order(mine, swap(mine, "dp", dp_bits[0]), core))
        means = jnp.concatenate(fresh, axis=1)
    return means, loss


def solution(mesh):
    placed = (P(("dp", "cent"), None), P(("dp", "cent"), None), P("cent", None), P(), P())
    return jax.shard_map(
        on_device,
        mesh=mesh,
        in_specs=placed,
        out_specs=(P("cent", None), P(("dp", "cent"))),
        check_vma=False,
    )
```

```python
import jax
import jax.numpy as jnp
from jax import lax
from jax.sharding import PartitionSpec as P

BLOCK = 128
ITERS = 2
SHARPNESS = 0.05
SCALE = 0.05
PRIOR = 1.0
FAR = -1e30


def swap(value, axis, bit):
    size = lax.axis_size(axis)
    return lax.ppermute(value, axis, [(i, i ^ bit) for i in range(size)])


def bits_of(size):
    return [1 << k for k in range(size.bit_length() - 1)]


def in_order(mine, other, flag):
    return jnp.concatenate([jnp.where(flag == 0, mine, other), jnp.where(flag == 0, other, mine)])


def column_pieces(value, later, axis, size):
    far = size // 2
    pieces = {0: later}
    for mask in sorted(range(2, size, 2), key=lambda m: (bin(m).count("1"), -m)):
        low = mask & -mask
        pieces[mask] = swap(value if mask == far else pieces[mask ^ low], axis, low)
    return pieces


def in_three(value):
    parts = []
    for _ in range(3):
        top = lax.reduce_precision(value, 8, 7)
        parts.append(top.astype(jnp.bfloat16))
        value = value - top
    return parts


def join_lse(first, second):
    top = jnp.maximum(first, second)
    return top + jnp.log(1.0 + jnp.exp(jnp.minimum(first, second) - top))


def on_device(passages, queries, init_centroids, pattern, positive_offset):
    n_dp, n_cent = lax.axis_size("dp"), lax.axis_size("cent")
    dp, cent = lax.axis_index("dp"), lax.axis_index("cent")
    dp_bits, cent_bits = bits_of(n_dp), bits_of(n_cent)
    core = dp & 1
    rows, width = passages.shape
    own_queries = queries.shape[0]
    half = n_cent // 2

    asked = swap(queries, "dp", dp_bits[0])
    asked, later, means = lax.optimization_barrier((asked, passages, init_centroids))

    evens = list(range(0, n_cent, 2))
    pieces = column_pieces(passages, later, "cent", n_cent)
    far = evens[half // 2]
    late, pieces[2] = lax.optimization_barrier((pieces[far], pieces[2]))
    across = {mask: swap(late if mask == far else pieces[mask], "cent", 1) for mask in evens[:-1]}
    asked = in_order(queries, asked, core)
    for bit in dp_bits[1:]:
        asked = in_order(asked, swap(asked, "dp", bit), dp & bit)
    pieces[2], pieces[0] = lax.optimization_barrier((pieces[2], passages))
    pieces[evens[-1]], asked = lax.optimization_barrier((pieces[evens[-1]], asked))
    held = [jnp.concatenate([pieces[mask] for mask in evens])]

    centers = means.shape[0]
    kept = centers // 2
    first = core == 0
    norms = jnp.sum(means * means, axis=1)
    centers_half = means.astype(jnp.bfloat16)
    packed = jnp.where(first, centers_half[:kept], centers_half[kept:])
    line = jnp.where(first, norms[:kept], norms[kept:])
    packed = jnp.concatenate([packed, jnp.pad(jnp.stack(in_three(line)), ((0, 5), (0, width - kept)))])
    mine = swap(packed, "cent", 1)
    other = swap(mine, "dp", dp_bits[0])
    partner_half = in_order(mine[:kept], other[:kept], core)
    lines = [part[kept : kept + 3, :kept].astype(jnp.float32) for part in (mine, other)]
    partner_norms = in_order(*[(three[0] + three[1]) + three[2] for three in lines], core)

    def loss_partials(asked, pattern, positive_offset, dp, cent):
        mine = (n_dp, n_cent, own_queries)
        picks = lax.dynamic_index_in_dim(pattern.reshape(mine + (-1,)), cent, 1, keepdims=False)
        picks = picks.reshape(n_dp * own_queries, -1)
        offset = lax.dynamic_index_in_dim(positive_offset.reshape(mine), cent, 1, keepdims=False).reshape(-1)
        target = picks[:, 0] * BLOCK + offset
        partials, positive = [], 0.0
        for index, group in enumerate(held):
            masks = jnp.array(evens, jnp.int32) | index
            owner = (dp * n_cent + (cent ^ masks)) * rows
            column = (owner[:, None] + jnp.arange(rows, dtype=jnp.int32)[None, :]).reshape(-1)
            scores = SCALE * lax.dot_general(
                asked, group, (((1,), (1,)), ((), ())), preferred_element_type=jnp.float32
            )
            allowed = jnp.any(picks[:, :, None] == (column // BLOCK)[None, None, :], axis=1)
            top = jnp.max(jnp.where(allowed, scores, FAR), axis=1)
            total = jnp.sum(jnp.where(allowed, jnp.exp(scores - top[:, None]), 0.0), axis=1)
            partials.append(jnp.where(total > 0.0, top + jnp.log(jnp.maximum(total, 1e-37)), FAR))
            positive = positive + jnp.sum(jnp.where(column[None, :] == target[:, None], scores, 0.0), axis=1)
        return positive, join_lse(*partials)

    def logits_of(centers_half, norms, group):
        products = lax.dot_general(centers_half, group, (((1,), (1,)), ((), ())), preferred_element_type=jnp.float32)
        return SHARPNESS * (2.0 * products - norms[:, None])

    def stats_of(*logits):
        top = jnp.max(logits[0], axis=0)
        for more in logits[1:]:
            top = jnp.maximum(top, jnp.max(more, axis=0))
        return top + jnp.log(sum(jnp.sum(jnp.exp(part - top[None, :]), axis=0) for part in logits))

    def over_column(bit, lse):
        axis = 0 if bit == 1 else len(cent_bits) - cent_bits.index(bit)
        return join_lse(lse, jnp.flip(swap(lse, "cent", bit), axis=axis))

    asks = n_dp * own_queries
    for step in range(ITERS):
        last = step == ITERS - 1
        shape = (-1,) + (2,) * (len(cent_bits) - 1) + (rows,)
        if step == 0:
            early = jnp.concatenate([pieces[mask] for mask in evens[:-1]])
            lse = [
                stats_of(logits_of(centers_half, norms, group), logits_of(partner_half, partner_norms, group))
                for group in (early, pieces[evens[-1]])
            ]
            lse = jnp.concatenate(lse).reshape(shape)
            lse, held[0] = lax.optimization_barrier((lse, held[0]))
            across[evens[-1]] = swap(held[0][-rows:], "cent", 1)
            stops = [0, half // 4, half // 2, half]
            for index, bit in enumerate(cent_bits[1:] + [None]):
                ties = evens[stops[index] : stops[index + 1]] if index < 3 else []
                lse, *parts = lax.optimization_barrier([lse] + [across[mask] for mask in ties])
                across.update(zip(ties, parts))
                if bit is not None:
                    lse = over_column(bit, lse)
                if index == 0:
                    lse, held[0] = lax.optimization_barrier((lse, held[0]))
                    odds = [logits_of(centers_half, norms, held[0])]
            held.append(jnp.concatenate([across[mask] for mask in evens]))
            lse = jnp.concatenate([lse, swap(lse, "cent", 1)])
            odds.append(logits_of(centers_half, norms, held[-1]))
            lse, odds = lax.optimization_barrier((lse, odds))
        else:
            norms = jnp.sum(means * means, axis=1)
            centers_half = means.astype(jnp.bfloat16)
            odds = [logits_of(centers_half, norms, group) for group in held]
            lse = jnp.concatenate([stats_of(part) for part in odds]).reshape(shape)
            for bit in cent_bits:
                lse = over_column(bit, lse)
                if last and bit == cent_bits[0]:
                    inputs = (lse, asked, pattern, positive_offset, dp, cent)
                    lse, *inputs = lax.optimization_barrier(inputs)
                    positive, found = loss_partials(*inputs)
        lse = lse.reshape(2, half * rows)
        resps, counts = [], 0.0
        for index in range(2):
            resp = jnp.exp(odds[index] - lse[index][None, :])
            counts = counts + jnp.sum(resp, axis=1)
            resps.append(resp.astype(jnp.bfloat16))

        line = jnp.where(first, counts[:kept], counts[kept:])
        rest = jnp.where(first, counts[kept:], counts[:kept])
        if last:
            line = jnp.concatenate([line, positive, found])
            rest = jnp.concatenate([rest, positive, found])

        def join_lines(line, other):
            cut = kept + asks
            if not last:
                return line + other
            return jnp.concatenate([line[:cut] + other[:cut], join_lse(line[cut:], other[cut:])])

        cut = width // 2
        totals = []
        for part in range(2):
            numer = 0.0
            for index in range(2):
                numer = numer + jnp.dot(
                    resps[index], held[index][:, part * cut : (part + 1) * cut], preferred_element_type=jnp.float32
                )
            total = jnp.where(first, numer[:kept], numer[kept:])
            sent = jnp.where(first, numer[kept:], numer[:kept])
            if part == 0:
                sent = jnp.concatenate([sent, jnp.pad(rest[None, :], ((0, 7), (0, cut - rest.shape[0])))])
            if part == 0:
                resps, _ = lax.optimization_barrier((resps, sent))
            other = swap(sent, "dp", dp_bits[0])
            totals.append(total + other[:kept])
            if part == 0:
                line = join_lines(line, other[kept, : line.shape[0]])
        for bit in dp_bits[1:]:
            for part in range(2):
                sent = totals[part]
                if isinstance(sent, tuple):
                    sent = sent[0].astype(jnp.float32) + sent[1].astype(jnp.float32)
                sent = sent.astype(jnp.bfloat16)
                packed = sent
                if part == 0:
                    parts = jnp.pad(jnp.stack(in_three(line)), ((0, 5), (0, cut - line.shape[0])))
                    packed = jnp.concatenate([packed, parts])
                    packed = jnp.pad(packed, ((0, -packed.shape[0] % 8), (0, 0)))
                other = swap(packed, "dp", bit)
                totals[part] = (sent, other[:kept])
                if part == 0:
                    three = other[kept : kept + 3, : line.shape[0]].astype(jnp.float32)
                    line = join_lines(line, (three[0] + three[1]) + three[2])
        if last:
            whole = line[kept + asks :] - line[kept : kept + asks]
            loss = lax.dynamic_slice_in_dim(whole, dp * own_queries, own_queries, 0)
        prior = jnp.where(first, means[:kept], means[kept:])
        fresh = []
        for part in range(2):
            mine = totals[part][0].astype(jnp.float32) + totals[part][1].astype(jnp.float32)
            mine = (mine + PRIOR * prior[:, part * cut : (part + 1) * cut]) / (line[:kept, None] + PRIOR)
            if part == 0:
                totals[1], _ = lax.optimization_barrier((totals[1], mine))
            fresh.append(in_order(mine, swap(mine, "dp", dp_bits[0]), core))
        means = jnp.concatenate(fresh, axis=1)
    return means, loss


def solution(mesh):
    placed = (P(("dp", "cent"), None), P(("dp", "cent"), None), P("cent", None), P(), P())
    return jax.shard_map(
        on_device,
        mesh=mesh,
        in_specs=placed,
        out_specs=(P("cent", None), P(("dp", "cent"))),
        check_vma=False,
    )
```

```python
import jax
import jax.numpy as jnp
from jax import lax
from jax.sharding import PartitionSpec as P

BLOCK = 128
ITERS = 2
SHARPNESS = 0.05
SCALE = 0.05
PRIOR = 1.0
FAR = -1e30


def swap(value, axis, bit):
    size = lax.axis_size(axis)
    return lax.ppermute(value, axis, [(i, i ^ bit) for i in range(size)])


def bits_of(size):
    return [1 << k for k in range(size.bit_length() - 1)]


def in_order(mine, other, flag):
    return jnp.concatenate([jnp.where(flag == 0, mine, other), jnp.where(flag == 0, other, mine)])


def column_pieces(value, later, axis, size):
    far = size // 2
    pieces = {0: later}
    for mask in sorted(range(2, size, 2), key=lambda m: (bin(m).count("1"), -m)):
        low = mask & -mask
        pieces[mask] = swap(value if mask == far else pieces[mask ^ low], axis, low)
    return pieces


def in_three(value):
    parts = []
    for _ in range(3):
        top = lax.reduce_precision(value, 8, 7)
        parts.append(top.astype(jnp.bfloat16))
        value = value - top
    return parts


def join_lse(first, second):
    top = jnp.maximum(first, second)
    return top + jnp.log(1.0 + jnp.exp(jnp.minimum(first, second) - top))


def on_device(passages, queries, init_centroids, pattern, positive_offset):
    n_dp, n_cent = lax.axis_size("dp"), lax.axis_size("cent")
    dp, cent = lax.axis_index("dp"), lax.axis_index("cent")
    dp_bits, cent_bits = bits_of(n_dp), bits_of(n_cent)
    core = dp & 1
    rows, width = passages.shape
    own_queries = queries.shape[0]
    half = n_cent // 2

    asked = swap(queries, "dp", dp_bits[0])
    asked, later, means = lax.optimization_barrier((asked, passages, init_centroids))

    evens = list(range(0, n_cent, 2))
    pieces = column_pieces(passages, later, "cent", n_cent)
    far = evens[half // 2]
    late, pieces[2] = lax.optimization_barrier((pieces[far], pieces[2]))
    across = {mask: swap(late if mask == far else pieces[mask], "cent", 1) for mask in evens[:-1]}
    asked = in_order(queries, asked, core)
    for bit in dp_bits[1:]:
        asked = in_order(asked, swap(asked, "dp", bit), dp & bit)
    pieces[2], pieces[0] = lax.optimization_barrier((pieces[2], passages))
    pieces[evens[-1]], asked = lax.optimization_barrier((pieces[evens[-1]], asked))
    held = [jnp.concatenate([pieces[mask] for mask in evens])]

    centers = means.shape[0]
    kept = centers // 2
    first = core == 0
    norms = jnp.sum(means * means, axis=1)
    centers_half = means.astype(jnp.bfloat16)
    packed = jnp.where(first, centers_half[:kept], centers_half[kept:])
    line = jnp.where(first, norms[:kept], norms[kept:])
    packed = jnp.concatenate([packed, jnp.pad(jnp.stack(in_three(line)), ((0, 5), (0, width - kept)))])
    mine = swap(packed, "cent", 1)
    other = swap(mine, "dp", dp_bits[0])
    partner_half = in_order(mine[:kept], other[:kept], core)
    lines = [part[kept : kept + 3, :kept].astype(jnp.float32) for part in (mine, other)]
    partner_norms = in_order(*[(three[0] + three[1]) + three[2] for three in lines], core)

    def loss_partials(asked, pattern, positive_offset, dp, cent):
        mine = (n_dp, n_cent, own_queries)
        picks = lax.dynamic_index_in_dim(pattern.reshape(mine + (-1,)), cent, 1, keepdims=False)
        picks = picks.reshape(n_dp * own_queries, -1)
        offset = lax.dynamic_index_in_dim(positive_offset.reshape(mine), cent, 1, keepdims=False).reshape(-1)
        target = picks[:, 0] * BLOCK + offset
        partials, positive = [], 0.0
        for index, group in enumerate(held):
            masks = jnp.array(evens, jnp.int32) | index
            owner = (dp * n_cent + (cent ^ masks)) * rows
            column = (owner[:, None] + jnp.arange(rows, dtype=jnp.int32)[None, :]).reshape(-1)
            scores = SCALE * lax.dot_general(
                asked, group, (((1,), (1,)), ((), ())), preferred_element_type=jnp.float32
            )
            allowed = jnp.any(picks[:, :, None] == (column // BLOCK)[None, None, :], axis=1)
            top = jnp.max(jnp.where(allowed, scores, FAR), axis=1)
            total = jnp.sum(jnp.where(allowed, jnp.exp(scores - top[:, None]), 0.0), axis=1)
            partials.append(jnp.where(total > 0.0, top + jnp.log(jnp.maximum(total, 1e-37)), FAR))
            positive = positive + jnp.sum(jnp.where(column[None, :] == target[:, None], scores, 0.0), axis=1)
        return positive, join_lse(*partials)

    def logits_of(centers_half, norms, group):
        products = lax.dot_general(centers_half, group, (((1,), (1,)), ((), ())), preferred_element_type=jnp.float32)
        return SHARPNESS * (2.0 * products - norms[:, None])

    def stats_of(*logits):
        top = jnp.max(logits[0], axis=0)
        for more in logits[1:]:
            top = jnp.maximum(top, jnp.max(more, axis=0))
        return top + jnp.log(sum(jnp.sum(jnp.exp(part - top[None, :]), axis=0) for part in logits))

    def over_column(bit, lse):
        axis = 0 if bit == 1 else len(cent_bits) - cent_bits.index(bit)
        return join_lse(lse, jnp.flip(swap(lse, "cent", bit), axis=axis))

    asks = n_dp * own_queries
    for step in range(ITERS):
        last = step == ITERS - 1
        shape = (-1,) + (2,) * (len(cent_bits) - 1) + (rows,)
        if step == 0:
            early = jnp.concatenate([pieces[mask] for mask in evens[:-1]])
            lse = [
                stats_of(logits_of(centers_half, norms, group), logits_of(partner_half, partner_norms, group))
                for group in (early, pieces[evens[-1]])
            ]
            lse = jnp.concatenate(lse).reshape(shape)
            lse, held[0] = lax.optimization_barrier((lse, held[0]))
            across[evens[-1]] = swap(held[0][-rows:], "cent", 1)
            stops = [0, half // 4, half // 2, half]
            for index, bit in enumerate(cent_bits[1:] + [None]):
                ties = evens[stops[index] : stops[index + 1]] if index < 3 else []
                lse, *parts = lax.optimization_barrier([lse] + [across[mask] for mask in ties])
                across.update(zip(ties, parts))
                if bit is not None:
                    lse = over_column(bit, lse)
                if index == 0:
                    lse, held[0] = lax.optimization_barrier((lse, held[0]))
                    odds = [logits_of(centers_half, norms, held[0])]
            held.append(jnp.concatenate([across[mask] for mask in evens]))
            lse = jnp.concatenate([lse, swap(lse, "cent", 1)])
            odds.append(logits_of(centers_half, norms, held[-1]))
            lse, odds = lax.optimization_barrier((lse, odds))
        else:
            norms = jnp.sum(means * means, axis=1)
            centers_half = means.astype(jnp.bfloat16)
            odds = [logits_of(centers_half, norms, group) for group in held]
            lse = jnp.concatenate([stats_of(part) for part in odds]).reshape(shape)
            for bit in cent_bits:
                lse = over_column(bit, lse)
                if last and bit == cent_bits[0]:
                    inputs = (lse, asked, pattern, positive_offset, dp, cent)
                    lse, *inputs = lax.optimization_barrier(inputs)
                    positive, found = loss_partials(*inputs)
        lse = lse.reshape(2, half * rows)
        resps, counts = [], 0.0
        for index in range(2):
            resp = jnp.exp(odds[index] - lse[index][None, :])
            counts = counts + jnp.sum(resp, axis=1)
            resps.append(resp.astype(jnp.bfloat16))

        line = jnp.where(first, counts[:kept], counts[kept:])
        rest = jnp.where(first, counts[kept:], counts[:kept])
        if last:
            line = jnp.concatenate([line, positive, found])
            rest = jnp.concatenate([rest, positive, found])

        def join_lines(line, other):
            cut = kept + asks
            if not last:
                return line + other
            return jnp.concatenate([line[:cut] + other[:cut], join_lse(line[cut:], other[cut:])])

        cut = width // 2

        def lines_of(line):
            return jnp.pad(jnp.stack(in_three(line)), ((0, 5), (0, cut - line.shape[0])))

        def line_of(packed, count):
            three = packed[kept : kept + 3, :count].astype(jnp.float32)
            return (three[0] + three[1]) + three[2]

        totals = []
        for part in range(2):
            numer = 0.0
            for index in range(2):
                numer = numer + jnp.dot(
                    resps[index], held[index][:, part * cut : (part + 1) * cut], preferred_element_type=jnp.float32
                )
            total = jnp.where(first, numer[:kept], numer[kept:])
            sent = jnp.where(first, numer[kept:], numer[:kept])
            sent = sent.astype(jnp.bfloat16)
            if part == 0:
                sent = jnp.concatenate([sent, lines_of(rest)])
                resps, _ = lax.optimization_barrier((resps, sent))
            other = swap(sent, "dp", dp_bits[0])
            totals.append(total + other[:kept].astype(jnp.float32))
            if part == 0:
                line = join_lines(line, line_of(other, line.shape[0]))
        for bit in dp_bits[1:]:
            for part in range(2):
                sent = totals[part]
                if isinstance(sent, tuple):
                    sent = sent[0].astype(jnp.float32) + sent[1].astype(jnp.float32)
                sent = sent.astype(jnp.bfloat16)
                packed = sent
                if part == 0:
                    packed = jnp.concatenate([packed, lines_of(line)])
                other = swap(packed, "dp", bit)
                totals[part] = (sent, other[:kept])
                if part == 0:
                    line = join_lines(line, line_of(other, line.shape[0]))
        if last:
            whole = line[kept + asks :] - line[kept : kept + asks]
            loss = lax.dynamic_slice_in_dim(whole, dp * own_queries, own_queries, 0)
        prior = jnp.where(first, means[:kept], means[kept:])
        fresh = []
        for part in range(2):
            mine = totals[part][0].astype(jnp.float32) + totals[part][1].astype(jnp.float32)
            mine = (mine + PRIOR * prior[:, part * cut : (part + 1) * cut]) / (line[:kept, None] + PRIOR)
            if part == 0:
                totals[1], _ = lax.optimization_barrier((totals[1], mine))
            fresh.append(in_order(mine, swap(mine, "dp", dp_bits[0]), core))
        means = jnp.concatenate(fresh, axis=1)
    return means, loss


def solution(mesh):
    placed = (P(("dp", "cent"), None), P(("dp", "cent"), None), P("cent", None), P(), P())
    return jax.shard_map(
        on_device,
        mesh=mesh,
        in_specs=placed,
        out_specs=(P("cent", None), P(("dp", "cent"))),
        check_vma=False,
    )
```

```python
import jax
import jax.numpy as jnp
from jax import lax
from jax.sharding import PartitionSpec as P

BLOCK = 128
ITERS = 2
SHARPNESS = 0.05
SCALE = 0.05
PRIOR = 1.0
FAR = -1e30


def swap(value, axis, bit):
    size = lax.axis_size(axis)
    return lax.ppermute(value, axis, [(i, i ^ bit) for i in range(size)])


def bits_of(size):
    return [1 << k for k in range(size.bit_length() - 1)]


def in_order(mine, other, flag):
    return jnp.concatenate([jnp.where(flag == 0, mine, other), jnp.where(flag == 0, other, mine)])


def column_pieces(value, later, axis, size):
    far = size // 2
    pieces = {0: later}
    for mask in sorted(range(2, size, 2), key=lambda m: (bin(m).count("1"), -m)):
        low = mask & -mask
        pieces[mask] = swap(value if mask == far else pieces[mask ^ low], axis, low)
    return pieces


def in_three(value):
    parts = []
    for _ in range(3):
        top = lax.reduce_precision(value, 8, 7)
        parts.append(top.astype(jnp.bfloat16))
        value = value - top
    return parts


def join_lse(first, second):
    top = jnp.maximum(first, second)
    return top + jnp.log(1.0 + jnp.exp(jnp.minimum(first, second) - top))


def on_device(passages, queries, init_centroids, pattern, positive_offset):
    n_dp, n_cent = lax.axis_size("dp"), lax.axis_size("cent")
    dp, cent = lax.axis_index("dp"), lax.axis_index("cent")
    dp_bits, cent_bits = bits_of(n_dp), bits_of(n_cent)
    core = dp & 1
    rows, width = passages.shape
    own_queries = queries.shape[0]
    half = n_cent // 2

    asked = swap(queries, "dp", dp_bits[0])
    asked, later, means = lax.optimization_barrier((asked, passages, init_centroids))

    evens = list(range(0, n_cent, 2))
    pieces = column_pieces(passages, later, "cent", n_cent)
    far = evens[half // 2]
    late, pieces[2] = lax.optimization_barrier((pieces[far], pieces[2]))
    across = {mask: swap(late if mask == far else pieces[mask], "cent", 1) for mask in evens[:-1]}
    asked = in_order(queries, asked, core)
    for bit in dp_bits[1:]:
        asked = in_order(asked, swap(asked, "dp", bit), dp & bit)
    pieces[2], pieces[0] = lax.optimization_barrier((pieces[2], passages))
    pieces[evens[-1]], asked = lax.optimization_barrier((pieces[evens[-1]], asked))
    held = [jnp.concatenate([pieces[mask] for mask in evens])]

    centers = means.shape[0]
    kept = centers // 2
    first = core == 0
    norms = jnp.sum(means * means, axis=1)
    centers_half = means.astype(jnp.bfloat16)
    packed = jnp.where(first, centers_half[:kept], centers_half[kept:])
    line = jnp.where(first, norms[:kept], norms[kept:])
    packed = jnp.concatenate([packed, jnp.pad(jnp.stack(in_three(line)), ((0, 5), (0, width - kept)))])
    mine = swap(packed, "cent", 1)
    other = swap(mine, "dp", dp_bits[0])
    partner_half = in_order(mine[:kept], other[:kept], core)
    lines = [part[kept : kept + 3, :kept].astype(jnp.float32) for part in (mine, other)]
    partner_norms = in_order(*[(three[0] + three[1]) + three[2] for three in lines], core)

    def loss_partials(asked, pattern, positive_offset, dp, cent):
        mine = (n_dp, n_cent, own_queries)
        picks = lax.dynamic_index_in_dim(pattern.reshape(mine + (-1,)), cent, 1, keepdims=False)
        picks = picks.reshape(n_dp * own_queries, -1)
        offset = lax.dynamic_index_in_dim(positive_offset.reshape(mine), cent, 1, keepdims=False).reshape(-1)
        target = picks[:, 0] * BLOCK + offset
        partials, positive = [], 0.0
        for index, group in enumerate(held):
            masks = jnp.array(evens, jnp.int32) | index
            owner = (dp * n_cent + (cent ^ masks)) * rows
            column = (owner[:, None] + jnp.arange(rows, dtype=jnp.int32)[None, :]).reshape(-1)
            scores = SCALE * lax.dot_general(
                asked, group, (((1,), (1,)), ((), ())), preferred_element_type=jnp.float32
            )
            allowed = jnp.any(picks[:, :, None] == (column // BLOCK)[None, None, :], axis=1)
            top = jnp.max(jnp.where(allowed, scores, FAR), axis=1)
            total = jnp.sum(jnp.where(allowed, jnp.exp(scores - top[:, None]), 0.0), axis=1)
            partials.append(jnp.where(total > 0.0, top + jnp.log(jnp.maximum(total, 1e-37)), FAR))
            positive = positive + jnp.sum(jnp.where(column[None, :] == target[:, None], scores, 0.0), axis=1)
        return positive, join_lse(*partials)

    def logits_of(centers_half, norms, group):
        products = lax.dot_general(centers_half, group, (((1,), (1,)), ((), ())), preferred_element_type=jnp.float32)
        return SHARPNESS * (2.0 * products - norms[:, None])

    def stats_of(*logits):
        top = jnp.max(logits[0], axis=0)
        for more in logits[1:]:
            top = jnp.maximum(top, jnp.max(more, axis=0))
        return top + jnp.log(sum(jnp.sum(jnp.exp(part - top[None, :]), axis=0) for part in logits))

    def over_column(bit, lse):
        axis = 0 if bit == 1 else len(cent_bits) - cent_bits.index(bit)
        return join_lse(lse, jnp.flip(swap(lse, "cent", bit), axis=axis))

    asks = n_dp * own_queries
    for step in range(ITERS):
        last = step == ITERS - 1
        shape = (-1,) + (2,) * (len(cent_bits) - 1) + (rows,)
        if step == 0:
            early = jnp.concatenate([pieces[mask] for mask in evens[:-1]])
            lse = [
                stats_of(logits_of(centers_half, norms, group), logits_of(partner_half, partner_norms, group))
                for group in (early, pieces[evens[-1]])
            ]
            lse = jnp.concatenate(lse).reshape(shape)
            lse, held[0] = lax.optimization_barrier((lse, held[0]))
            across[evens[-1]] = swap(held[0][-rows:], "cent", 1)
            stops = [0, half // 4, half // 2, half]
            for index, bit in enumerate(cent_bits[1:] + [None]):
                ties = evens[stops[index] : stops[index + 1]] if index < 3 else []
                lse, *parts = lax.optimization_barrier([lse] + [across[mask] for mask in ties])
                across.update(zip(ties, parts))
                if bit is not None:
                    lse = over_column(bit, lse)
                if index == 0:
                    lse, held[0] = lax.optimization_barrier((lse, held[0]))
                    odds = [logits_of(centers_half, norms, held[0])]
            held.append(jnp.concatenate([across[mask] for mask in evens]))
            lse = jnp.concatenate([lse, swap(lse, "cent", 1)])
            odds.append(logits_of(centers_half, norms, held[-1]))
            lse, odds = lax.optimization_barrier((lse, odds))
        else:
            norms = jnp.sum(means * means, axis=1)
            centers_half = means.astype(jnp.bfloat16)
            odds = [logits_of(centers_half, norms, group) for group in held]
            lse = jnp.concatenate([stats_of(part) for part in odds]).reshape(shape)
            hops = cent_bits[::-1]
            for bit in hops:
                lse = over_column(bit, lse)
                if last and bit == hops[0]:
                    inputs = (lse, asked, pattern, positive_offset, dp, cent)
                    lse, *inputs = lax.optimization_barrier(inputs)
                    positive, found = loss_partials(*inputs)
        lse = lse.reshape(2, half * rows)
        resps, counts = [], 0.0
        for index in range(2):
            resp = jnp.exp(odds[index] - lse[index][None, :])
            counts = counts + jnp.sum(resp, axis=1)
            resps.append(resp.astype(jnp.bfloat16))

        line = jnp.where(first, counts[:kept], counts[kept:])
        rest = jnp.where(first, counts[kept:], counts[:kept])
        if last:
            line = jnp.concatenate([line, positive, found])
            rest = jnp.concatenate([rest, positive, found])

        def join_lines(line, other):
            cut = kept + asks
            if not last:
                return line + other
            return jnp.concatenate([line[:cut] + other[:cut], join_lse(line[cut:], other[cut:])])

        cut = width // 2

        def lines_of(line):
            return jnp.pad(jnp.stack(in_three(line)), ((0, 5), (0, cut - line.shape[0])))

        def line_of(packed, count):
            three = packed[kept : kept + 3, :count].astype(jnp.float32)
            return (three[0] + three[1]) + three[2]

        totals = []
        for part in range(2):
            numer = 0.0
            for index in range(2):
                numer = numer + jnp.dot(
                    resps[index], held[index][:, part * cut : (part + 1) * cut], preferred_element_type=jnp.float32
                )
            total = jnp.where(first, numer[:kept], numer[kept:])
            sent = jnp.where(first, numer[kept:], numer[:kept])
            sent = sent.astype(jnp.bfloat16)
            if part == 0:
                sent = jnp.concatenate([sent, lines_of(rest)])
                resps, _ = lax.optimization_barrier((resps, sent))
            other = swap(sent, "dp", dp_bits[0])
            totals.append(total + other[:kept].astype(jnp.float32))
            if part == 0:
                line = join_lines(line, line_of(other, line.shape[0]))
        for bit in dp_bits[1:]:
            for part in range(2):
                sent = totals[part]
                if isinstance(sent, tuple):
                    sent = sent[0].astype(jnp.float32) + sent[1].astype(jnp.float32)
                sent = sent.astype(jnp.bfloat16)
                packed = sent
                if part == 0:
                    packed = jnp.concatenate([packed, lines_of(line)])
                other = swap(packed, "dp", bit)
                totals[part] = (sent, other[:kept])
                if part == 0:
                    line = join_lines(line, line_of(other, line.shape[0]))
        if last:
            whole = line[kept + asks :] - line[kept : kept + asks]
            loss = lax.dynamic_slice_in_dim(whole, dp * own_queries, own_queries, 0)
        prior = jnp.where(first, means[:kept], means[kept:])
        fresh = []
        for part in range(2):
            mine = totals[part][0].astype(jnp.float32) + totals[part][1].astype(jnp.float32)
            mine = (mine + PRIOR * prior[:, part * cut : (part + 1) * cut]) / (line[:kept, None] + PRIOR)
            if part == 0:
                totals[1], _ = lax.optimization_barrier((totals[1], mine))
            fresh.append(in_order(mine, swap(mine, "dp", dp_bits[0]), core))
        means = jnp.concatenate(fresh, axis=1)
    return means, loss


def solution(mesh):
    placed = (P(("dp", "cent"), None), P(("dp", "cent"), None), P("cent", None), P(), P())
    return jax.shard_map(
        on_device,
        mesh=mesh,
        in_specs=placed,
        out_specs=(P("cent", None), P(("dp", "cent"))),
        check_vma=False,
    )
```
